128 devices in a mesh: ep: 4 (over z_hi, core), fsdp: 32 (over y, z_lo, x).
Axes of the slice: x: 4, y: 4, z: 4 (z_hi: 2, z_lo: 2; z = z_hi * 2 + z_lo), core: 2. Of those that a mesh axis runs over, the one named last changes fastest.
Arguments:
- gate_weight: bfloat16 [32, 4096, 1536], P('ep', 'fsdp'), may hold values from -0.09375 to 0.09375
- up_weight: bfloat16 [32, 4096, 1536], P('ep', 'fsdp'), may hold values from -0.09375 to 0.09375
- down_weight: bfloat16 [32, 4096, 1536], P('ep', 'fsdp'), may hold values from -0.09375 to 0.09375
- model_factors: bfloat16 [32, 3, 64, 4096], P('ep', None, None, 'fsdp'), may hold values from -0.09375 to 0.09375
- hidden_factors: bfloat16 [32, 3, 64, 1536], P('ep', None, 'fsdp'), may hold values from -0.75 to 0.75
- active: int32 [32], P('ep'), may hold values 0 or 1
- expert_rollout_slot: int32 [32], replicated, may hold values from 0 to 31, each once
Outputs:
- quantized: bfloat16 [32, 3, 4096, 1536], P('fsdp', None, None, 'ep')
- block_scales: bfloat16 [32, 3, 32, 12], P('fsdp', None, None, 'ep')
The draws below stay inside these ranges and needn't reach their ends.
Inputs may be any that keep to these rules, and one draw needn't show every extreme that they name: `expert_rollout_slot`: each slot number appears exactly once; slot s belongs to rollout owner s.
All inputs are finite; a program needn't handle non-finite values. No bound on the sum of `active` on one device may be relied on, other than what follows from the above.
Results may differ from the reference program's by a relative error of at most 0.004.
Values may be sent and summed in bfloat16 or wider, within the bound.
A program may use at most 128 MiB of HBM per device.

```python
import jax
import jax.numpy as jnp
from jax import lax

D = 4096
F = 1536
R = 64
BLK = 128
EXPERTS = 32


def touch_ends(drawn, key, least, largest):
    spot = [jax.random.randint(jax.random.fold_in(key, axis), (), 0, length) for axis, length in enumerate(drawn.shape)]
    widest = drawn.shape.index(max(drawn.shape))
    beside = spot[:widest] + [(spot[widest] + 1) % drawn.shape[widest]] + spot[widest + 1:]
    return drawn.at[tuple(spot)].set(least).at[tuple(beside)].set(largest)


def level_of(own_key, extent, cuts, least, top_value):
    level, own = 1.0, jax.random.fold_in(own_key, 6)
    for axis_at, parts in cuts:
        draws = jnp.exp(jax.random.uniform(jax.random.fold_in(own, axis_at), (parts,), jnp.float32, least / len(cuts), top_value / len(cuts)))
        level = level * jnp.repeat(draws, extent[axis_at] // parts).reshape([-1 if axis == axis_at else 1 for axis in range(len(extent))])
    return level


def gaussian(own_key, extent, deviation, most, shards=(), kind=jnp.bfloat16):
    entries = jax.random.normal(own_key, extent, jnp.float32) * deviation
    if len(shards) > 0:
        entries = level_of(own_key, extent, shards, -0.22, 0.18) * entries
    return jnp.clip(entries, min=-most, max=most).astype(kind)


def setup_inputs(seed: int = 0) -> dict:
    keys = jax.random.split(jax.random.key(seed), 8)
    gate_weight = gaussian(keys[0], (EXPERTS, D, F), D ** -0.5, 0.09375, ((0, 4), (1, 32)))
    up_weight = gaussian(keys[1], (EXPERTS, D, F), D ** -0.5, 0.09375, ((0, 4), (1, 32)))
    down_weight = gaussian(keys[2], (EXPERTS, D, F), D ** -0.5, 0.09375, ((0, 4), (1, 32)))
    model_factors = gaussian(keys[3], (EXPERTS, 3, R, D), D ** -0.5, 0.09375, ((0, 4), (3, 32)))
    hidden_factors = gaussian(keys[4], (EXPERTS, 3, R, F), R ** -0.5, 0.75, ((0, 4), (2, 32)))
    active = touch_ends((jax.random.randint(keys[5], (EXPERTS,), 0, 2) < 1).astype(jnp.int32), jax.random.fold_in(keys[5], 1), 0, 1)
    expert_rollout_slot = jax.random.permutation(keys[6], EXPERTS).astype(jnp.int32)
    return dict(gate_weight=gate_weight, up_weight=up_weight, down_weight=down_weight, model_factors=model_factors, hidden_factors=hidden_factors, active=active, expert_rollout_slot=expert_rollout_slot)


ADAPTER_SCALE = 2.0


def quantize(merged_weight):
    lead = merged_weight.shape[:-2]
    rows = merged_weight.shape[-2]
    cols = merged_weight.shape[-1]
    blocks = merged_weight.reshape(lead + (rows // BLK, BLK, cols // BLK, BLK))
    block_max = jnp.max(jnp.abs(blocks), axis=(-3, -1))
    scales = (block_max + 1e-6).astype(jnp.bfloat16)
    widened_values = lax.optimization_barrier(scales).astype(jnp.float32)
    values = (blocks / widened_values[..., :, None, :, None]).reshape(merged_weight.shape).astype(jnp.bfloat16)
    return values, scales


def reference(gate_weight, up_weight, down_weight, model_factors, hidden_factors, active, expert_rollout_slot):
    slots = jnp.arange(EXPERTS, dtype=jnp.int32)
    source = jnp.sum(jnp.where(expert_rollout_slot[None, :] == slots[:, None], slots[None, :], 0), axis=1).astype(jnp.int32)

    def one_slot(expert_index):
        expert_weights = jnp.stack([gate_weight[expert_index], up_weight[expert_index], down_weight[expert_index]]).astype(jnp.float32)
        adapter_update = jnp.einsum("prd,prf->pdf", model_factors[expert_index].astype(jnp.float32), hidden_factors[expert_index].astype(jnp.float32), precision=lax.Precision.HIGHEST)
        merged_weight = expert_weights + ADAPTER_SCALE * active[expert_index].astype(jnp.float32) * adapter_update
        return quantize(merged_weight)

    quantized, block_scales = lax.map(one_slot, source)
    return quantized, block_scales
```

```python
import jax
import jax.numpy as jnp
from jax import lax
from jax.experimental import pallas as pl
from jax.experimental.pallas import tpu as pltpu
from jax.sharding import PartitionSpec as P

BLK = 128
ADAPTER_SCALE = 2.0
EP = 4
OWNERS = 32
LOCAL = 8
EXPERTS = EP * LOCAL
MATS = 3
RANK = 64
COLS = 384
NCB = COLS // BLK
MF_ROWS = MATS * RANK
HF_ROWS = 32
AUX_ROWS = MF_ROWS + HF_ROWS
CHUNKS = tuple((p, cb, 1) for p in range(MATS) for cb in range(NCB))
LAG = 1
MESH = pl.DeviceIdType.MESH


def kernel(source, gate, up, down, mf, hfp, out, scales_out, *scratch):
    n = len(CHUNKS)
    a_bufs, b_bufs, l_bufs = scratch[: n + 1], scratch[n + 1 : 2 * n + 2], scratch[2 * n + 2 : 3 * n + 3]
    o_bufs, (hf_all, a_send, a_recv, b_send, b_recv, o_sem) = scratch[3 * n + 3 : 4 * n + 3], scratch[4 * n + 3 :]
    weights = (gate, up, down)

    k, j = lax.axis_index("ep"), lax.axis_index("fsdp")
    h = k // 2
    y, l, x = j // 8, (j // 4) % 2, j % 4
    flip = 4 - 8 * l

    def partner(d):
        k2 = (k + d) % EP
        dh = k2 // 2 - h
        return k2, j + dh * dh * flip

    def owner(o):
        return ((y + o // 8) % 4) * 8 + ((l + (o // 4) % 2) % 2) * 4 + (x + o % 4) % 4

    barrier = pltpu.get_barrier_semaphore()
    for d in range(1, EP):
        pl.semaphore_signal(barrier, inc=1, device_id=partner(d), device_id_type=MESH)

    @pl.loop(1, OWNERS)
    def _(o):
        pl.semaphore_signal(barrier, inc=1, device_id=(k, owner(o)), device_id_type=MESH)

    pl.semaphore_wait(barrier, EP - 1 + OWNERS - 1)

    mine = pl.ds(k * LOCAL, LOCAL)

    def a_pairs(c, k2):
        if c == n:
            return (
                (mf, a_bufs[n].at[mine, pl.ds(0, MF_ROWS), :]),
                (hfp.at[:, k2], a_bufs[n].at[mine, pl.ds(MF_ROWS, HF_ROWS), :]),
            )
        p, cb, m = CHUNKS[c]
        columns = pl.ds(pl.multiple_of(k2 * COLS + cb * BLK, BLK), m * BLK)
        return ((weights[p].at[:, :, columns], a_bufs[c].at[mine]),)

    def a_start(c):
        for d in range(1, EP):
            k2, j2 = partner(d)
            for src, dst in a_pairs(c, k2):
                pltpu.make_async_remote_copy(
                    src_ref=src, dst_ref=dst, send_sem=a_send.at[c], recv_sem=a_recv.at[c],
                    device_id=(k2, j2), device_id_type=MESH,
                ).start()
        for src, dst in a_pairs(c, k):
            pltpu.make_async_copy(src, dst, a_recv.at[c]).start()

    def b_start(c):
        a, b, land = a_bufs[c], b_bufs[c], l_bufs[c]

        @pl.loop(0, OWNERS)
        def _(s):
            b[s] = a[source[s]]

        @pl.loop(1, OWNERS)
        def _(o):
            s = owner(o)
            pltpu.make_async_remote_copy(
                src_ref=b.at[s], dst_ref=land.at[j], send_sem=b_send.at[c], recv_sem=b_recv.at[c],
                device_id=(k, s), device_id_type=MESH,
            ).start()

        pltpu.make_async_copy(b.at[j], land.at[j], b_recv.at[c]).start()

    order = (n,) + tuple(range(n))
    for c in order:
        a_start(c)

    crossed = source[j] // (2 * LOCAL) - h
    crossed = crossed * crossed

    def factors():
        pltpu.make_async_copy(l_bufs[n], l_bufs[n], b_recv.at[n]).wait()
        packed = l_bufs[n][:, MF_ROWS:, :].reshape(OWNERS * HF_ROWS, BLK)
        row = lax.broadcasted_iota(jnp.int32, (RANK, OWNERS * HF_ROWS), 0)
        col = lax.broadcasted_iota(jnp.int32, (RANK, OWNERS * HF_ROWS), 1)
        holder = row // 2
        holder = holder + crossed * (4 - 8 * ((holder // 4) % 2))
        first = holder * HF_ROWS + (row % 2) * NCB
        for p in range(MATS):
            for cb in range(NCB):
                pick = jnp.where(col == first + (p * 2 * NCB + cb), 1.0, 0.0).astype(jnp.bfloat16)
                hf_all[p, :, cb * BLK : (cb + 1) * BLK] = jnp.dot(
                    pick, packed, preferred_element_type=jnp.float32
                ).astype(jnp.bfloat16)

    def compute(c):
        p, cb0, m = CHUNKS[c]
        pltpu.make_async_copy(l_bufs[c], l_bufs[c], b_recv.at[c]).wait()
        land, aux, o_buf = l_bufs[c], l_bufs[n], o_bufs[c]

        @pl.loop(0, OWNERS, unroll=4)
        def _(i):
            held = i + crossed * (4 - 8 * ((i // 4) % 2))
            delta = lax.dot_general(
                aux[held, p * RANK : (p + 1) * RANK, :],
                hf_all[p, :, cb0 * BLK : (cb0 + m) * BLK],
                (((0,), (0,)), ((), ())),
                preferred_element_type=jnp.float32,
            )
            merged = land[held].astype(jnp.float32) + delta
            for q in range(m):
                block = merged[:, q * BLK : (q + 1) * BLK]
                most = jnp.max(jnp.max(jnp.abs(block), axis=0, keepdims=True), axis=1, keepdims=True)
                scale = (most + 1e-6).astype(jnp.bfloat16).astype(jnp.float32)
                o_buf[i, :, q * BLK : (q + 1) * BLK] = (block * (1.0 / scale)).astype(jnp.bfloat16)
                scales_out[p * NCB + cb0 + q, pl.ds(i, 1), :] = jnp.broadcast_to(scale, (1, BLK))

        pltpu.make_async_copy(o_buf, out.at[p, :, :, pl.ds(cb0 * BLK, m * BLK)], o_sem.at[c]).start()

    done = 0
    for at, c in enumerate(order):
        pltpu.make_async_copy(a_bufs[c], a_bufs[c], a_recv.at[c]).wait()
        b_start(c)
        while done < at - LAG:
            if done == 0:
                factors()
            compute(done)
            done += 1
    while done < n:
        if done == 0:
            factors()
        compute(done)
        done += 1

    for c in range(n + 1):
        given = a_bufs[c].at[pl.ds(0, EXPERTS - LOCAL)]
        pltpu.make_async_copy(given, given, a_send.at[c]).wait()
        given = b_bufs[c].at[pl.ds(0, OWNERS - 1)]
        pltpu.make_async_copy(given, given, b_send.at[c]).wait()
    for c, (p, cb0, m) in enumerate(CHUNKS):
        pltpu.make_async_copy(o_bufs[c], out.at[p, :, :, pl.ds(cb0 * BLK, m * BLK)], o_sem.at[c]).wait()


def on_device(
    gate_weight, up_weight, down_weight, model_factors, hidden_factors, active, expert_rollout_slot
):
    n = len(CHUNKS)
    slots = jnp.arange(EXPERTS, dtype=jnp.int32)
    source = jnp.sum(
        jnp.where(expert_rollout_slot[None, :] == slots[:, None], slots[None, :], 0), axis=1
    ).astype(jnp.int32)
    mf = model_factors.reshape(LOCAL, MF_ROWS, BLK)
    factor = (ADAPTER_SCALE * active.astype(jnp.float32)).astype(jnp.bfloat16)
    hf = hidden_factors * factor[:, None, None, None]
    hfp = hf.reshape(LOCAL, MATS * 2, EP, NCB, BLK).transpose(0, 2, 1, 3, 4)
    hfp = hfp.reshape(LOCAL, EP, MATS * 2 * NCB, BLK)
    hfp = jnp.pad(hfp, ((0, 0), (0, 0), (0, HF_ROWS - MATS * 2 * NCB), (0, 0)))

    def bufs():
        shapes = [(OWNERS, BLK, m * BLK) for _, _, m in CHUNKS] + [(OWNERS, AUX_ROWS, BLK)]
        return [pltpu.VMEM(shape, jnp.bfloat16) for shape in shapes]

    quantized, scales = pl.pallas_call(
        kernel,
        out_shape=(
            jax.ShapeDtypeStruct((MATS, OWNERS, BLK, COLS), jnp.bfloat16),
            jax.ShapeDtypeStruct((MATS * NCB, OWNERS, BLK), jnp.float32),
        ),
        in_specs=[pl.BlockSpec(memory_space=pltpu.SMEM)] + [pl.BlockSpec(memory_space=pl.ANY)] * 5,
        out_specs=(pl.BlockSpec(memory_space=pl.ANY), pl.BlockSpec(memory_space=pltpu.VMEM)),
        scratch_shapes=bufs() + bufs() + bufs() + bufs()[:n] + [
            pltpu.VMEM((MATS, RANK, COLS), jnp.bfloat16),
            pltpu.SemaphoreType.DMA((n + 1,)),
            pltpu.SemaphoreType.DMA((n + 1,)),
            pltpu.SemaphoreType.DMA((n + 1,)),
            pltpu.SemaphoreType.DMA((n + 1,)),
            pltpu.SemaphoreType.DMA((n,)),
        ],
        compiler_params=pltpu.CompilerParams(
            collective_id=0, has_side_effects=True, vmem_limit_bytes=60 * 1024 * 1024
        ),
    )(source, gate_weight, up_weight, down_weight, mf, hfp)
    quantized = quantized.reshape(1, MATS, OWNERS * BLK, COLS)
    block_scales = scales[:, :, 0].reshape(MATS, NCB, OWNERS).transpose(0, 2, 1)
    return quantized, block_scales[None].astype(jnp.bfloat16)


def solution(mesh):
    placed = (
        P("ep", "fsdp", None),
        P("ep", "fsdp", None),
        P("ep", "fsdp", None),
        P("ep", None, None, "fsdp"),
        P("ep", None, "fsdp", None),
        P("ep"),
        P(),
    )
    return jax.shard_map(
        on_device,
        mesh=mesh,
        in_specs=placed,
        out_specs=(P("fsdp", None, None, "ep"), P("fsdp", None, None, "ep")),
        check_vma=False,
    )
```

```python
import jax
import jax.numpy as jnp
from jax import lax
from jax.experimental import pallas as pl
from jax.experimental.pallas import tpu as pltpu
from jax.sharding import PartitionSpec as P

BLK = 128
ADAPTER_SCALE = 2
EP = 4
OWNERS = 32
LOCAL = 8
EXPERTS = EP * LOCAL
MATS = 3
RANK = 64
HALF = RANK // 2
COLS = 384
NCB = COLS // BLK
BLOCKS = MATS * NCB
ROWS = ((64, 64),) + ((128,),) * 7 + ((64, 64),)
PIECES = tuple(
    (b, sum(cut[:i]), rows) for b, cut in enumerate(ROWS) for i, rows in enumerate(cut)
)
AUX = len(PIECES)
AUX_AT = 2
ORDER = tuple(range(AUX_AT)) + (AUX,) + tuple(range(AUX_AT, AUX))
LAG = 2
STEP = 13
MESH = pl.DeviceIdType.MESH


def kernel(active, slot, gate, up, down, mf, hf, out, scales_out, *scratch):
    n = AUX + 1
    a_bufs, b_bufs, l_bufs = scratch[:n], scratch[n : 2 * n], scratch[2 * n : 3 * n]
    (hf_in, hf_wide, hf_rows, sibling, hf_all, source,
     a_send, a_recv, b_send, b_recv, c_send, c_recv, in_sem) = scratch[3 * n :]
    weights = (gate, up, down)

    k, j = lax.axis_index("ep"), lax.axis_index("fsdp")
    h, core = k // 2, k % 2
    y, l, x = j // 8, (j // 4) % 2, j % 4
    flip = 4 - 8 * l

    def partner(d):
        k2 = (k + d) % EP
        dh = k2 // 2 - h
        return k2, j + dh * dh * flip

    def owner(o):
        o = (o * STEP) % OWNERS
        return ((y + o // 8) % 4) * 8 + ((l + (o // 4) % 2) % 2) * 4 + (x + o % 4) % 4

    barrier = pltpu.get_barrier_semaphore()
    for d in range(1, EP):
        pl.semaphore_signal(barrier, inc=1, device_id=partner(d), device_id_type=MESH)

    @pl.loop(1, OWNERS)
    def _(o):
        pl.semaphore_signal(barrier, inc=1, device_id=(k, owner(o)), device_id_type=MESH)

    hf_copy = pltpu.make_async_copy(hf, hf_in, in_sem)
    hf_copy.start()
    pl.semaphore_wait(barrier, EP - 1 + OWNERS - 1)

    mine = pl.ds(k * LOCAL, LOCAL)

    def a_pairs(c, k2):
        if c == AUX:
            return (
                (mf.at[:, :, pl.ds((k2 % 2) * HALF, HALF), :], a_bufs[c].at[mine, pl.ds(0, MATS)]),
                (hf_rows.at[:, pl.ds(k2, 1)], a_bufs[c].at[mine, pl.ds(MATS, 1)]),
            )
        b, r0, rows = PIECES[c]
        columns = pl.ds(pl.multiple_of(k2 * COLS + (b % NCB) * BLK, BLK), BLK)
        return ((weights[b // NCB].at[:, pl.ds(r0, rows), columns], a_bufs[c].at[mine]),)

    def a_start(c):
        for d in range(1, EP):
            k2, j2 = partner(d)
            for src, dst in a_pairs(c, k2):
                pltpu.make_async_remote_copy(
                    src_ref=src, dst_ref=dst, send_sem=a_send.at[c], recv_sem=a_recv.at[c],
                    device_id=(k2, j2), device_id_type=MESH,
                ).start()
        for src, dst in a_pairs(c, k):
            pltpu.make_async_copy(src, dst, a_recv.at[c]).start()

    def b_start(c):
        a, b, land = a_bufs[c], b_bufs[c], l_bufs[c]

        @pl.loop(0, OWNERS)
        def _(s):
            b[s] = a[source[s]]

        @pl.loop(1, OWNERS)
        def _(o):
            s = owner(o)
            pltpu.make_async_remote_copy(
                src_ref=b.at[s], dst_ref=land.at[j], send_sem=b_send.at[c], recv_sem=b_recv.at[c],
                device_id=(k, s), device_id_type=MESH,
            ).start()

        pltpu.make_async_copy(b.at[j], land.at[j], b_recv.at[c]).start()

    for c in ORDER[:AUX_AT]:
        a_start(c)

    hf_copy.wait()

    @pl.loop(0, LOCAL)
    def _(e):
        factor = (ADAPTER_SCALE * active[e]).astype(jnp.float32)
        for k2 in range(EP):
            hf_wide[k2] = jnp.zeros((HALF, BLK), jnp.float32)
        for p in range(MATS):
            rows = hf_in[e, p].astype(jnp.float32) * factor
            for k2 in range(EP):
                for cb in range(NCB):
                    at = k2 * COLS + cb * BLK
                    hf_wide[k2, pl.ds(2 * (p * NCB + cb), 2), :] = rows[:, at : at + BLK]
        hf_rows[e] = hf_wide[...].astype(jnp.bfloat16)

    for c in ORDER[AUX_AT:]:
        a_start(c)

    @pl.loop(0, OWNERS)
    def _(s):
        found = jnp.int32(0)
        for e in range(EXPERTS):
            found = jnp.where(slot[e] == s, e, found)
        source[s] = found

    crossed = source[j] // (2 * LOCAL) - h
    crossed = crossed * crossed

    def sibling_copy():
        return pltpu.make_async_remote_copy(
            src_ref=l_bufs[AUX].at[:, pl.ds(0, MATS)], dst_ref=sibling, send_sem=c_send, recv_sem=c_recv,
            device_id=(k + 1 - 2 * core, j), device_id_type=MESH,
        )

    def b_wait(c):
        pltpu.make_async_copy(l_bufs[c], l_bufs[c], b_recv.at[c]).wait()

    def factors():
        b_wait(AUX)
        sibling_copy().start()
        packed = l_bufs[AUX][:, MATS].reshape(OWNERS * HALF, BLK)
        row = lax.broadcasted_iota(jnp.int32, (RANK, OWNERS * HALF), 0)
        col = lax.broadcasted_iota(jnp.int32, (RANK, OWNERS * HALF), 1)
        row = (row + core * HALF) % RANK
        holder = row // 2
        holder = holder + crossed * (4 - 8 * ((holder // 4) % 2))
        first = holder * HALF + row % 2
        for p in range(MATS):
            for cb in range(NCB):
                pick = jnp.where(col == first + 2 * (p * NCB + cb), 1.0, 0.0).astype(jnp.bfloat16)
                hf_all[p * NCB + cb] = jnp.dot(pick, packed, preferred_element_type=jnp.float32).astype(jnp.bfloat16)

    lanes = lax.broadcasted_iota(jnp.int32, (1, BLK), 1)

    def compute(b):
        pieces = [c for c in range(AUX) if PIECES[c][0] == b]
        for c in pieces:
            b_wait(c)
        aux, p = l_bufs[AUX], b // NCB

        def one(i, scales):
            held = i + crossed * (4 - 8 * ((i // 4) % 2))
            delta = lax.dot_general(
                jnp.concatenate([aux[held, p], sibling[held, p]], axis=0),
                hf_all[b],
                (((0,), (0,)), ((), ())),
                preferred_element_type=jnp.float32,
            )
            raw = [l_bufs[c][held].astype(jnp.float32) for c in pieces]
            merged = (raw[0] if len(raw) == 1 else jnp.concatenate(raw, axis=0)) + delta
            most = jnp.max(jnp.max(jnp.abs(merged), axis=0, keepdims=True), axis=1, keepdims=True)
            scale = (most + 1e-6).astype(jnp.bfloat16).astype(jnp.float32)
            out[b, i] = (merged * (1.0 / scale)).astype(jnp.bfloat16)
            return jnp.where(lanes == i, scale, scales)

        scales = lax.fori_loop(0, OWNERS, one, jnp.zeros((1, BLK), jnp.float32), unroll=4)
        scales_out[p, pl.ds(b % NCB, 1), :] = scales

    todo = [(ORDER.index(AUX), "factors")]
    todo += [(max(ORDER.index(c) for c in range(AUX) if PIECES[c][0] == b), b) for b in range(BLOCKS)]

    def work(until):
        while todo and todo[0][0] <= until:
            task = todo.pop(0)[1]
            if task == "factors":
                factors()
                continue
            if task == 0:
                sibling_copy().wait()
            compute(task)

    for at, c in enumerate(ORDER):
        pltpu.make_async_copy(a_bufs[c], a_bufs[c], a_recv.at[c]).wait()
        b_start(c)
        work(at - LAG)
    work(len(ORDER))

    for c in range(n):
        given = a_bufs[c].at[pl.ds(0, EXPERTS - LOCAL)]
        pltpu.make_async_copy(given, given, a_send.at[c]).wait()
        given = b_bufs[c].at[pl.ds(0, OWNERS - 1)]
        pltpu.make_async_copy(given, given, b_send.at[c]).wait()


def store(blocks, scales, out, scales_out, sem):
    copies = [
        pltpu.make_async_copy(
            blocks.at[b], out.at[b // NCB, :, :, pl.ds((b % NCB) * BLK, BLK)], sem.at[b]
        )
        for b in range(BLOCKS)
    ]
    for copy in copies:
        copy.start()
    for p in range(MATS):
        scales_out[p] = scales[p, :NCB, :OWNERS].astype(jnp.bfloat16)
    for copy in copies:
        copy.wait()


def on_device(
    gate_weight, up_weight, down_weight, model_factors, hidden_factors, active, expert_rollout_slot
):
    shapes = [(OWNERS, rows, BLK) for _, _, rows in PIECES] + [(OWNERS, MATS + 1, HALF, BLK)]
    bufs = [pltpu.VMEM(shape, jnp.bfloat16) for shape in shapes]
    smem, vmem, anywhere = (pl.BlockSpec(memory_space=s) for s in (pltpu.SMEM, pltpu.VMEM, pl.ANY))
    sems = pltpu.SemaphoreType.DMA
    n = len(bufs)

    blocks, scales = pl.pallas_call(
        kernel,
        out_shape=(
            pltpu.VMEM((BLOCKS, OWNERS, BLK, BLK), jnp.bfloat16),
            pltpu.VMEM((MATS, 8, BLK), jnp.float32),
        ),
        in_specs=[smem, smem] + [anywhere] * 5,
        out_specs=(vmem, vmem),
        scratch_shapes=bufs * 3 + [
            pltpu.VMEM((LOCAL, MATS, 2, EP * COLS), jnp.bfloat16),
            pltpu.VMEM((EP, HALF, BLK), jnp.float32),
            pltpu.VMEM((LOCAL, EP, HALF, BLK), jnp.bfloat16),
            pltpu.VMEM((OWNERS, MATS, HALF, BLK), jnp.bfloat16),
            pltpu.VMEM((BLOCKS, RANK, BLK), jnp.bfloat16),
            pltpu.SMEM((EXPERTS,), jnp.int32),
            sems((n,)), sems((n,)), sems((n,)), sems((n,)), sems, sems, sems,
        ],
        compiler_params=pltpu.CompilerParams(
            collective_id=0, has_side_effects=True, vmem_limit_bytes=46 * 1024 * 1024
        ),
    )(active, expert_rollout_slot, gate_weight, up_weight, down_weight, model_factors, hidden_factors)

    quantized, block_scales = pl.pallas_call(
        store,
        out_shape=(
            jax.ShapeDtypeStruct((MATS, OWNERS, BLK, COLS), jnp.bfloat16),
            jax.ShapeDtypeStruct((MATS, NCB, OWNERS), jnp.bfloat16),
        ),
        in_specs=[anywhere, vmem],
        out_specs=(anywhere, vmem),
        scratch_shapes=[sems((BLOCKS,))],
        compiler_params=pltpu.CompilerParams(vmem_limit_bytes=4 * 1024 * 1024),
    )(blocks, scales)
    return quantized.reshape(1, MATS, OWNERS * BLK, COLS), block_scales.transpose(0, 2, 1)[None]


def solution(mesh):
    placed = (
        P("ep", "fsdp", None),
        P("ep", "fsdp", None),
        P("ep", "fsdp", None),
        P("ep", None, None, "fsdp"),
        P("ep", None, "fsdp", None),
        P("ep"),
        P(),
    )
    return jax.shard_map(
        on_device,
        mesh=mesh,
        in_specs=placed,
        out_specs=(P("fsdp", None, None, "ep"), P("fsdp", None, None, "ep")),
        check_vma=False,
    )
```

```python
import jax
import jax.numpy as jnp
from jax import lax
from jax.experimental import pallas as pl
from jax.experimental.pallas import tpu as pltpu
from jax.sharding import PartitionSpec as P

BLK = 128
ADAPTER_SCALE = 2
EP = 4
OWNERS = 32
LOCAL = 8
EXPERTS = EP * LOCAL
MATS = 3
RANK = 64
HALF = RANK // 2
COLS = 384
NCB = COLS // BLK
BLOCKS = MATS * NCB
ROWS = ((64, 64),) + ((128,),) * 7 + ((64, 64),)
PIECES = tuple(
    (b, sum(cut[:i]), rows) for b, cut in enumerate(ROWS) for i, rows in enumerate(cut)
)
AUX = len(PIECES)
AUX_AT = 2
ORDER = tuple(range(AUX_AT)) + (AUX,) + tuple(range(AUX_AT, AUX))
LAG = 2
LAST = BLOCKS - 1
LAST_PIECES = tuple(c for c in range(AUX) if PIECES[c][0] == LAST)
STORE = 8
STEP = 13
MESH = pl.DeviceIdType.MESH


def crossing(home):
    away = home // (2 * LOCAL) - lax.axis_index("ep") // 2
    return away * away


def merge(i, crossed, aux, sibling, factors, pieces, p):
    held = i + crossed * (4 - 8 * ((i // 4) % 2))
    delta = lax.dot_general(
        jnp.concatenate([aux[held, p], sibling[held, p]], axis=0),
        factors,
        (((0,), (0,)), ((), ())),
        preferred_element_type=jnp.float32,
    )
    raw = [piece[held].astype(jnp.float32) for piece in pieces]
    merged = (raw[0] if len(raw) == 1 else jnp.concatenate(raw, axis=0)) + delta
    most = jnp.max(jnp.max(jnp.abs(merged), axis=0, keepdims=True), axis=1, keepdims=True)
    scale = (most + 1e-6).astype(jnp.bfloat16).astype(jnp.float32)
    return (merged * (1.0 / scale)).astype(jnp.bfloat16), scale


def kernel(active, slot, gate, up, down, mf, hf, out, scales_out, hf_all, sibling, *refs):
    n = AUX + 1
    kept, refs = refs[: len(LAST_PIECES) + 1], refs[len(LAST_PIECES) + 1 :]
    first = n - len(kept)
    a_bufs, b_bufs, l_bufs = refs[:n], refs[n : 2 * n], refs[2 * n : 2 * n + first] + kept
    (hf_in, hf_wide, hf_rows, source,
     a_send, a_recv, b_send, b_recv, c_send, c_recv, in_sem) = refs[2 * n + first :]
    weights = (gate, up, down)

    k, j = lax.axis_index("ep"), lax.axis_index("fsdp")
    h, core = k // 2, k % 2
    y, l, x = j // 8, (j // 4) % 2, j % 4
    flip = 4 - 8 * l

    def partner(d):
        k2 = (k + d) % EP
        dh = k2 // 2 - h
        return k2, j + dh * dh * flip

    def owner(o):
        o = (o * STEP) % OWNERS
        return ((y + o // 8) % 4) * 8 + ((l + (o // 4) % 2) % 2) * 4 + (x + o % 4) % 4

    barrier = pltpu.get_barrier_semaphore()
    for d in range(1, EP):
        pl.semaphore_signal(barrier, inc=1, device_id=partner(d), device_id_type=MESH)

    @pl.loop(1, OWNERS)
    def _(o):
        pl.semaphore_signal(barrier, inc=1, device_id=(k, owner(o)), device_id_type=MESH)

    hf_copy = pltpu.make_async_copy(hf, hf_in, in_sem)
    hf_copy.start()
    pl.semaphore_wait(barrier, EP - 1 + OWNERS - 1)

    mine = pl.ds(k * LOCAL, LOCAL)

    def a_pairs(c, k2):
        if c == AUX:
            return (
                (mf.at[:, :, pl.ds((k2 % 2) * HALF, HALF), :], a_bufs[c].at[mine, pl.ds(0, MATS)]),
                (hf_rows.at[:, pl.ds(k2, 1)], a_bufs[c].at[mine, pl.ds(MATS, 1)]),
            )
        b, r0, rows = PIECES[c]
        columns = pl.ds(pl.multiple_of(k2 * COLS + (b % NCB) * BLK, BLK), BLK)
        return ((weights[b // NCB].at[:, pl.ds(r0, rows), columns], a_bufs[c].at[mine]),)

    def a_start(c):
        for d in range(1, EP):
            k2, j2 = partner(d)
            for src, dst in a_pairs(c, k2):
                pltpu.make_async_remote_copy(
                    src_ref=src, dst_ref=dst, send_sem=a_send.at[c], recv_sem=a_recv.at[c],
                    device_id=(k2, j2), device_id_type=MESH,
                ).start()
        for src, dst in a_pairs(c, k):
            pltpu.make_async_copy(src, dst, a_recv.at[c]).start()

    def b_start(c):
        a, b, land = a_bufs[c], b_bufs[c], l_bufs[c]

        @pl.loop(0, OWNERS)
        def _(s):
            b[s] = a[source[s]]

        @pl.loop(1, OWNERS)
        def _(o):
            s = owner(o)
            pltpu.make_async_remote_copy(
                src_ref=b.at[s], dst_ref=land.at[j], send_sem=b_send.at[c], recv_sem=b_recv.at[c],
                device_id=(k, s), device_id_type=MESH,
            ).start()

        pltpu.make_async_copy(b.at[j], land.at[j], b_recv.at[c]).start()

    for c in ORDER[:AUX_AT]:
        a_start(c)

    hf_copy.wait()

    @pl.loop(0, LOCAL)
    def _(e):
        factor = (ADAPTER_SCALE * active[e]).astype(jnp.float32)
        for k2 in range(EP):
            hf_wide[k2] = jnp.zeros((HALF, BLK), jnp.float32)
        for p in range(MATS):
            rows = hf_in[e, p].astype(jnp.float32) * factor
            for k2 in range(EP):
                for cb in range(NCB):
                    at = k2 * COLS + cb * BLK
                    hf_wide[k2, pl.ds(2 * (p * NCB + cb), 2), :] = rows[:, at : at + BLK]
        hf_rows[e] = hf_wide[...].astype(jnp.bfloat16)

    for c in ORDER[AUX_AT:]:
        a_start(c)

    @pl.loop(0, OWNERS)
    def _(s):
        found = jnp.int32(0)
        for e in range(EXPERTS):
            found = jnp.where(slot[e] == s, e, found)
        source[s] = found

    crossed = crossing(source[j])

    def sibling_copy():
        return pltpu.make_async_remote_copy(
            src_ref=l_bufs[AUX].at[:, pl.ds(0, MATS)], dst_ref=sibling, send_sem=c_send, recv_sem=c_recv,
            device_id=(k + 1 - 2 * core, j), device_id_type=MESH,
        )

    def b_wait(c):
        pltpu.make_async_copy(l_bufs[c], l_bufs[c], b_recv.at[c]).wait()

    def factors():
        b_wait(AUX)
        sibling_copy().start()
        packed = l_bufs[AUX][:, MATS].reshape(OWNERS * HALF, BLK)
        row = lax.broadcasted_iota(jnp.int32, (RANK, OWNERS * HALF), 0)
        col = lax.broadcasted_iota(jnp.int32, (RANK, OWNERS * HALF), 1)
        row = (row + core * HALF) % RANK
        holder = row // 2
        holder = holder + crossed * (4 - 8 * ((holder // 4) % 2))
        first = holder * HALF + row % 2
        for p in range(MATS):
            for cb in range(NCB):
                pick = jnp.where(col == first + 2 * (p * NCB + cb), 1.0, 0.0).astype(jnp.bfloat16)
                hf_all[p * NCB + cb] = jnp.dot(pick, packed, preferred_element_type=jnp.float32).astype(jnp.bfloat16)

    lanes = lax.broadcasted_iota(jnp.int32, (1, BLK), 1)

    def compute(b):
        pieces = [c for c in range(AUX) if PIECES[c][0] == b]
        for c in pieces:
            b_wait(c)
        if b == LAST:
            return
        p, columns = b // NCB, slice((b % NCB) * BLK, (b % NCB + 1) * BLK)

        def one(i, scales):
            out[p, i, :, columns], scale = merge(
                i, crossed, l_bufs[AUX], sibling, hf_all[b], [l_bufs[c] for c in pieces], p
            )
            return jnp.where(lanes == i, scale, scales)

        scales = lax.fori_loop(0, OWNERS, one, jnp.zeros((1, BLK), jnp.float32), unroll=4)
        scales_out[p, pl.ds(b % NCB, 1), :] = scales

    todo = [(ORDER.index(AUX), "factors")]
    todo += [(max(ORDER.index(c) for c in range(AUX) if PIECES[c][0] == b), b) for b in range(BLOCKS)]

    def work(until):
        while todo and todo[0][0] <= until:
            task = todo.pop(0)[1]
            if task == "factors":
                factors()
                continue
            if task == 0:
                sibling_copy().wait()
            compute(task)

    for at, c in enumerate(ORDER):
        pltpu.make_async_copy(a_bufs[c], a_bufs[c], a_recv.at[c]).wait()
        b_start(c)
        work(at - LAG)
    work(len(ORDER))

    for c in range(n):
        given = a_bufs[c].at[pl.ds(0, EXPERTS - LOCAL)]
        pltpu.make_async_copy(given, given, a_send.at[c]).wait()
        given = b_bufs[c].at[pl.ds(0, OWNERS - 1)]
        pltpu.make_async_copy(given, given, b_send.at[c]).wait()


def store(slot, blocks, scales, hf_all, sibling, *refs):
    pieces, aux = refs[: len(LAST_PIECES)], refs[len(LAST_PIECES)]
    out, scales_out, last, sem = refs[len(LAST_PIECES) + 1 :]
    p, cb = LAST // NCB, LAST % NCB
    copies = []

    def begin(src, dst):
        copies.append(pltpu.make_async_copy(src, dst, sem.at[len(copies)]))
        copies[-1].start()

    for q in range(MATS):
        for i in range(0, OWNERS, STORE):
            rows = pl.ds(i, STORE)
            if q == p:
                begin(blocks.at[q, rows, :, pl.ds(0, cb * BLK)], out.at[q, rows, :, pl.ds(0, cb * BLK)])
            else:
                begin(blocks.at[q, rows], out.at[q, rows])

    j = lax.axis_index("fsdp")
    home = jnp.int32(0)
    for e in range(EXPERTS):
        home = jnp.where(slot[e] == j, e, home)
    crossed = crossing(home)
    lanes = lax.broadcasted_iota(jnp.int32, (1, BLK), 1)

    def one(i, scales_now):
        last[i], scale = merge(i, crossed, aux, sibling, hf_all[LAST], pieces, p)
        return jnp.where(lanes == i, scale, scales_now)

    final = jnp.zeros((1, BLK), jnp.float32)
    for i in range(0, OWNERS, STORE):
        final = lax.fori_loop(i, i + STORE, one, final, unroll=4)
        rows = pl.ds(i, STORE)
        begin(last.at[rows], out.at[p, rows, :, pl.ds(cb * BLK, BLK)])
    for q in range(MATS):
        scales_out[q] = scales[q, :NCB, :OWNERS].astype(jnp.bfloat16)
    scales_out[p, cb : cb + 1, :] = final[:, :OWNERS].astype(jnp.bfloat16)
    for copy in copies:
        copy.wait()


def on_device(
    gate_weight, up_weight, down_weight, model_factors, hidden_factors, active, expert_rollout_slot
):
    shapes = [(OWNERS, rows, BLK) for _, _, rows in PIECES] + [(OWNERS, MATS + 1, HALF, BLK)]
    bufs = [pltpu.VMEM(shape, jnp.bfloat16) for shape in shapes]
    smem, vmem, anywhere = (pl.BlockSpec(memory_space=s) for s in (pltpu.SMEM, pltpu.VMEM, pl.ANY))
    sems = pltpu.SemaphoreType.DMA
    n = len(bufs)

    kept = len(LAST_PIECES) + 1
    made = pl.pallas_call(
        kernel,
        out_shape=(
            pltpu.VMEM((MATS, OWNERS, BLK, COLS), jnp.bfloat16),
            pltpu.VMEM((MATS, 8, BLK), jnp.float32),
            pltpu.VMEM((BLOCKS, RANK, BLK), jnp.bfloat16),
            pltpu.VMEM((OWNERS, MATS, HALF, BLK), jnp.bfloat16),
            *bufs[n - kept :],
        ),
        in_specs=[smem, smem] + [anywhere] * 5,
        out_specs=(vmem,) * (4 + kept),
        scratch_shapes=bufs * 2 + bufs[: n - kept] + [
            pltpu.VMEM((LOCAL, MATS, 2, EP * COLS), jnp.bfloat16),
            pltpu.VMEM((EP, HALF, BLK), jnp.float32),
            pltpu.VMEM((LOCAL, EP, HALF, BLK), jnp.bfloat16),
            pltpu.SMEM((EXPERTS,), jnp.int32),
            sems((n,)), sems((n,)), sems((n,)), sems((n,)), sems, sems, sems,
        ],
        compiler_params=pltpu.CompilerParams(
            collective_id=0, has_side_effects=True, vmem_limit_bytes=50 * 1024 * 1024
        ),
    )(active, expert_rollout_slot, gate_weight, up_weight, down_weight, model_factors, hidden_factors)

    quantized, block_scales = pl.pallas_call(
        store,
        out_shape=(
            jax.ShapeDtypeStruct((MATS, OWNERS, BLK, COLS), jnp.bfloat16),
            jax.ShapeDtypeStruct((MATS, NCB, OWNERS), jnp.bfloat16),
        ),
        in_specs=[smem, anywhere] + [vmem] * (3 + kept),
        out_specs=(anywhere, vmem),
        scratch_shapes=[pltpu.VMEM((OWNERS, BLK, BLK), jnp.bfloat16), sems(((MATS + 1) * OWNERS // STORE,))],
        compiler_params=pltpu.CompilerParams(vmem_limit_bytes=8 * 1024 * 1024),
    )(expert_rollout_slot, *made)
    return quantized.reshape(1, MATS, OWNERS * BLK, COLS), block_scales.transpose(0, 2, 1)[None]


def solution(mesh):
    placed = (
        P("ep", "fsdp", None),
        P("ep", "fsdp", None),
        P("ep", "fsdp", None),
        P("ep", None, None, "fsdp"),
        P("ep", None, "fsdp", None),
        P("ep"),
        P(),
    )
    return jax.shard_map(
        on_device,
        mesh=mesh,
        in_specs=placed,
        out_specs=(P("fsdp", None, None, "ep"), P("fsdp", None, None, "ep")),
        check_vma=False,
    )
```

```python
import jax
import jax.numpy as jnp
from jax import lax
from jax.experimental import pallas as pl
from jax.experimental.pallas import tpu as pltpu
from jax.sharding import PartitionSpec as P

BLK = 128
ADAPTER_SCALE = 2
EP = 4
OWNERS = 32
LOCAL = 8
EXPERTS = EP * LOCAL
MATS = 3
RANK = 64
HALF = RANK // 2
COLS = 384
NCB = COLS // BLK
BLOCKS = MATS * NCB
ROWS = ((64, 64),) + ((128,),) * 7 + ((64, 64),)
PIECES = tuple(
    (b, sum(cut[:i]), rows) for b, cut in enumerate(ROWS) for i, rows in enumerate(cut)
)
AUX = len(PIECES)
AUX_AT = 2
ORDER = tuple(range(AUX_AT)) + (AUX,) + tuple(range(AUX_AT, AUX))
LAG = 2
LAST = BLOCKS - 1
LAST_PIECES = tuple(c for c in range(AUX) if PIECES[c][0] == LAST)
STORE = 8
STEP = 13
MESH = pl.DeviceIdType.MESH


def crossing(home):
    away = home // (2 * LOCAL) - lax.axis_index("ep") // 2
    return away * away


def merge(i, crossed, aux, sibling, factors, pieces, p):
    held = i + crossed * (4 - 8 * ((i // 4) % 2))
    delta = lax.dot_general(
        jnp.concatenate([aux[held, p], sibling[held, p]], axis=0),
        factors,
        (((0,), (0,)), ((), ())),
        preferred_element_type=jnp.float32,
    )
    raw = [piece[held].astype(jnp.float32) for piece in pieces]
    merged = (raw[0] if len(raw) == 1 else jnp.concatenate(raw, axis=0)) + delta
    most = jnp.max(jnp.max(jnp.abs(merged), axis=0, keepdims=True), axis=1, keepdims=True)
    scale = (most + 1e-6).astype(jnp.bfloat16).astype(jnp.float32)
    return (merged * (1.0 / scale)).astype(jnp.bfloat16), scale


def kernel(active_in, slot_in, gate, up, down, mf, hf, out, scales_out, hf_all, sibling, *refs):
    n = AUX + 1
    kept, refs = refs[: len(LAST_PIECES) + 1], refs[len(LAST_PIECES) + 1 :]
    first = n - len(kept)
    a_bufs, b_bufs, l_bufs = refs[:n], refs[n : 2 * n], refs[2 * n : 2 * n + first] + kept
    (hf_in, hf_wide, hf_rows, active, slot, source,
     a_send, a_recv, b_send, b_recv, c_send, c_recv, in_sem) = refs[2 * n + first :]
    weights = (gate, up, down)

    k, j = lax.axis_index("ep"), lax.axis_index("fsdp")
    h, core = k // 2, k % 2
    y, l, x = j // 8, (j // 4) % 2, j % 4
    flip = 4 - 8 * l

    def partner(d):
        k2 = (k + d) % EP
        dh = k2 // 2 - h
        return k2, j + dh * dh * flip

    def owner(o):
        o = (o * STEP) % OWNERS
        return ((y + o // 8) % 4) * 8 + ((l + (o // 4) % 2) % 2) * 4 + (x + o % 4) % 4

    barrier = pltpu.get_barrier_semaphore()
    for d in range(1, EP):
        pl.semaphore_signal(barrier, inc=1, device_id=partner(d), device_id_type=MESH)

    @pl.loop(1, OWNERS, unroll=True)
    def _(o):
        pl.semaphore_signal(barrier, inc=1, device_id=(k, owner(o)), device_id_type=MESH)

    fetches = [
        pltpu.make_async_copy(src, dst, in_sem.at[q])
        for q, (src, dst) in enumerate(((hf, hf_in), (active_in, active), (slot_in, slot)))
    ]
    for fetch in fetches:
        fetch.start()
    pl.semaphore_wait(barrier, EP - 1 + OWNERS - 1)

    mine = pl.ds(k * LOCAL, LOCAL)

    def a_pairs(c, k2):
        if c == AUX:
            return (
                (mf.at[:, :, pl.ds((k2 % 2) * HALF, HALF), :], a_bufs[c].at[mine, pl.ds(0, MATS)]),
                (hf_rows.at[:, pl.ds(k2, 1)], a_bufs[c].at[mine, pl.ds(MATS, 1)]),
            )
        b, r0, rows = PIECES[c]
        columns = pl.ds(pl.multiple_of(k2 * COLS + (b % NCB) * BLK, BLK), BLK)
        return ((weights[b // NCB].at[:, pl.ds(r0, rows), columns], a_bufs[c].at[mine]),)

    def a_start(c):
        for d in range(1, EP):
            k2, j2 = partner(d)
            for src, dst in a_pairs(c, k2):
                pltpu.make_async_remote_copy(
                    src_ref=src, dst_ref=dst, send_sem=a_send.at[c], recv_sem=a_recv.at[c],
                    device_id=(k2, j2), device_id_type=MESH,
                ).start()
        for src, dst in a_pairs(c, k):
            pltpu.make_async_copy(src, dst, a_recv.at[c]).start()

    def b_start(c):
        a, b, land = a_bufs[c], b_bufs[c], l_bufs[c]

        @pl.loop(0, OWNERS)
        def _(s):
            b[s] = a[source[s]]

        @pl.loop(1, OWNERS)
        def _(o):
            s = owner(o)
            pltpu.make_async_remote_copy(
                src_ref=b.at[s], dst_ref=land.at[j], send_sem=b_send.at[c], recv_sem=b_recv.at[c],
                device_id=(k, s), device_id_type=MESH,
            ).start()

        pltpu.make_async_copy(b.at[j], land.at[j], b_recv.at[c]).start()

    for c in ORDER[:AUX_AT]:
        a_start(c)

    for fetch in fetches:
        fetch.wait()

    @pl.loop(0, LOCAL)
    def _(e):
        factor = (ADAPTER_SCALE * active[e]).astype(jnp.float32)
        for k2 in range(EP):
            hf_wide[k2] = jnp.zeros((HALF, BLK), jnp.float32)
        for p in range(MATS):
            rows = hf_in[e, p].astype(jnp.float32) * factor
            for k2 in range(EP):
                for cb in range(NCB):
                    at = k2 * COLS + cb * BLK
                    hf_wide[k2, pl.ds(2 * (p * NCB + cb), 2), :] = rows[:, at : at + BLK]
        hf_rows[e] = hf_wide[...].astype(jnp.bfloat16)

    for c in ORDER[AUX_AT:]:
        a_start(c)

    @pl.loop(0, OWNERS)
    def _(s):
        found = jnp.int32(0)
        for e in range(EXPERTS):
            found = jnp.where(slot[e] == s, e, found)
        source[s] = found

    crossed = crossing(source[j])

    def sibling_copy():
        return pltpu.make_async_remote_copy(
            src_ref=l_bufs[AUX].at[:, pl.ds(0, MATS)], dst_ref=sibling, send_sem=c_send, recv_sem=c_recv,
            device_id=(k + 1 - 2 * core, j), device_id_type=MESH,
        )

    def b_wait(c):
        pltpu.make_async_copy(l_bufs[c], l_bufs[c], b_recv.at[c]).wait()

    def factors():
        b_wait(AUX)
        sibling_copy().start()
        packed = l_bufs[AUX][:, MATS].reshape(OWNERS * HALF, BLK)
        row = lax.broadcasted_iota(jnp.int32, (RANK, OWNERS * HALF), 0)
        col = lax.broadcasted_iota(jnp.int32, (RANK, OWNERS * HALF), 1)
        row = (row + core * HALF) % RANK
        holder = row // 2
        holder = holder + crossed * (4 - 8 * ((holder // 4) % 2))
        first = holder * HALF + row % 2
        for p in range(MATS):
            for cb in range(NCB):
                pick = jnp.where(col == first + 2 * (p * NCB + cb), 1.0, 0.0).astype(jnp.bfloat16)
                hf_all[p * NCB + cb] = jnp.dot(pick, packed, preferred_element_type=jnp.float32).astype(jnp.bfloat16)

    lanes = lax.broadcasted_iota(jnp.int32, (1, BLK), 1)

    def compute(b):
        pieces = [c for c in range(AUX) if PIECES[c][0] == b]
        for c in pieces:
            b_wait(c)
        if b == LAST:
            return
        p, columns = b // NCB, slice((b % NCB) * BLK, (b % NCB + 1) * BLK)

        def one(i, scales):
            out[p, i, :, columns], scale = merge(
                i, crossed, l_bufs[AUX], sibling, hf_all[b], [l_bufs[c] for c in pieces], p
            )
            return jnp.where(lanes == i, scale, scales)

        scales = lax.fori_loop(0, OWNERS, one, jnp.zeros((1, BLK), jnp.float32), unroll=4)
        scales_out[p, pl.ds(b % NCB, 1), :] = scales

    todo = [(ORDER.index(AUX), "factors")]
    todo += [(max(ORDER.index(c) for c in range(AUX) if PIECES[c][0] == b), b) for b in range(BLOCKS)]

    def work(until):
        while todo and todo[0][0] <= until:
            task = todo.pop(0)[1]
            if task == "factors":
                factors()
                continue
            if task == 0:
                sibling_copy().wait()
            compute(task)

    for at, c in enumerate(ORDER):
        pltpu.make_async_copy(a_bufs[c], a_bufs[c], a_recv.at[c]).wait()
        b_start(c)
        work(at - LAG)

    def b_sent(c):
        given = b_bufs[c].at[pl.ds(0, OWNERS - 1)]
        pltpu.make_async_copy(given, given, b_send.at[c]).wait()

    for c in ORDER:
        given = a_bufs[c].at[pl.ds(0, EXPERTS - LOCAL)]
        pltpu.make_async_copy(given, given, a_send.at[c]).wait()
        if c not in LAST_PIECES:
            b_sent(c)
    work(len(ORDER))
    for c in LAST_PIECES:
        b_sent(c)


def store(slot_in, blocks, scales, hf_all, sibling, *refs):
    pieces, aux = refs[: len(LAST_PIECES)], refs[len(LAST_PIECES)]
    out, scales_out, slot, last, slot_sem, sem = refs[len(LAST_PIECES) + 1 :]
    p, cb = LAST // NCB, LAST % NCB
    copies = []
    fetch = pltpu.make_async_copy(slot_in, slot, slot_sem)
    fetch.start()

    def begin(src, dst):
        copies.append(pltpu.make_async_copy(src, dst, sem.at[len(copies)]))
        copies[-1].start()

    for q in range(MATS):
        for i in range(0, OWNERS, STORE):
            rows = pl.ds(i, STORE)
            if q == p:
                begin(blocks.at[q, rows, :, pl.ds(0, cb * BLK)], out.at[q, rows, :, pl.ds(0, cb * BLK)])
            else:
                begin(blocks.at[q, rows], out.at[q, rows])

    fetch.wait()
    j = lax.axis_index("fsdp")
    home = jnp.int32(0)
    for e in range(EXPERTS):
        home = jnp.where(slot[e] == j, e, home)
    crossed = crossing(home)
    lanes = lax.broadcasted_iota(jnp.int32, (1, BLK), 1)

    def one(i, scales_now):
        last[i], scale = merge(i, crossed, aux, sibling, hf_all[LAST], pieces, p)
        return jnp.where(lanes == i, scale, scales_now)

    final = jnp.zeros((1, BLK), jnp.float32)
    for i in range(0, OWNERS, STORE):
        final = lax.fori_loop(i, i + STORE, one, final, unroll=4)
        rows = pl.ds(i, STORE)
        begin(last.at[rows], out.at[p, rows, :, pl.ds(cb * BLK, BLK)])
    for q in range(MATS):
        scales_out[q] = scales[q, :NCB, :OWNERS].astype(jnp.bfloat16)
    scales_out[p, cb : cb + 1, :] = final[:, :OWNERS].astype(jnp.bfloat16)
    for copy in copies:
        copy.wait()


def on_device(
    gate_weight, up_weight, down_weight, model_factors, hidden_factors, active, expert_rollout_slot
):
    shapes = [(OWNERS, rows, BLK) for _, _, rows in PIECES] + [(OWNERS, MATS + 1, HALF, BLK)]
    bufs = [pltpu.VMEM(shape, jnp.bfloat16) for shape in shapes]
    vmem, anywhere = (pl.BlockSpec(memory_space=s) for s in (pltpu.VMEM, pl.ANY))
    sems = pltpu.SemaphoreType.DMA
    n = len(bufs)

    kept = len(LAST_PIECES) + 1
    made = pl.pallas_call(
        kernel,
        out_shape=(
            pltpu.VMEM((MATS, OWNERS, BLK, COLS), jnp.bfloat16),
            pltpu.VMEM((MATS, 8, BLK), jnp.float32),
            pltpu.VMEM((BLOCKS, RANK, BLK), jnp.bfloat16),
            pltpu.VMEM((OWNERS, MATS, HALF, BLK), jnp.bfloat16),
            *bufs[n - kept :],
        ),
        in_specs=[anywhere] * 7,
        out_specs=(vmem,) * (4 + kept),
        scratch_shapes=bufs * 2 + bufs[: n - kept] + [
            pltpu.VMEM((LOCAL, MATS, 2, EP * COLS), jnp.bfloat16),
            pltpu.VMEM((EP, HALF, BLK), jnp.float32),
            pltpu.VMEM((LOCAL, EP, HALF, BLK), jnp.bfloat16),
            pltpu.SMEM((LOCAL,), jnp.int32),
            pltpu.SMEM((EXPERTS,), jnp.int32),
            pltpu.SMEM((EXPERTS,), jnp.int32),
            sems((n,)), sems((n,)), sems((n,)), sems((n,)), sems, sems, sems((3,)),
        ],
        compiler_params=pltpu.CompilerParams(
            collective_id=0, has_side_effects=True, vmem_limit_bytes=50 * 1024 * 1024
        ),
    )(active, expert_rollout_slot, gate_weight, up_weight, down_weight, model_factors, hidden_factors)

    quantized, block_scales = pl.pallas_call(
        store,
        out_shape=(
            jax.ShapeDtypeStruct((MATS, OWNERS, BLK, COLS), jnp.bfloat16),
            jax.ShapeDtypeStruct((MATS, NCB, OWNERS), jnp.bfloat16),
        ),
        in_specs=[anywhere, anywhere] + [vmem] * (3 + kept),
        out_specs=(anywhere, vmem),
        scratch_shapes=[pltpu.SMEM((EXPERTS,), jnp.int32), pltpu.VMEM((OWNERS, BLK, BLK), jnp.bfloat16), sems, sems(((MATS + 1) * OWNERS // STORE,))],
        compiler_params=pltpu.CompilerParams(vmem_limit_bytes=8 * 1024 * 1024),
    )(expert_rollout_slot, *made)
    return quantized.reshape(1, MATS, OWNERS * BLK, COLS), block_scales.transpose(0, 2, 1)[None]


def solution(mesh):
    placed = (
        P("ep", "fsdp", None),
        P("ep", "fsdp", None),
        P("ep", "fsdp", None),
        P("ep", None, None, "fsdp"),
        P("ep", None, "fsdp", None),
        P("ep"),
        P(),
    )
    return jax.shard_map(
        on_device,
        mesh=mesh,
        in_specs=placed,
        out_specs=(P("fsdp", None, None, "ep"), P("fsdp", None, None, "ep")),
        check_vma=False,
    )
```

```python
import jax
import jax.numpy as jnp
from jax import lax
from jax.experimental import pallas as pl
from jax.experimental.pallas import tpu as pltpu
from jax.sharding import PartitionSpec as P

BLK = 128
ADAPTER_SCALE = 2
EP = 4
OWNERS = 32
LOCAL = 8
EXPERTS = EP * LOCAL
MATS = 3
RANK = 64
HALF = RANK // 2
COLS = 384
NCB = COLS // BLK
BLOCKS = MATS * NCB
ROWS = ((48, 48, 32),) * 9
PIECES = tuple(
    (b, sum(cut[:i]), rows) for b, cut in enumerate(ROWS) for i, rows in enumerate(cut)
)
AUX = len(PIECES)
FACTORS = (AUX, AUX + 1)
ALL = AUX + len(FACTORS)
AUX_AT = 2
ORDER = tuple(range(AUX_AT)) + FACTORS + tuple(range(AUX_AT, AUX))
LAG = 4
LAST = BLOCKS - 1
LAST_PIECES = tuple(c for c in range(AUX) if PIECES[c][0] == LAST)
STORE = 8
STEP = 13
MESH = pl.DeviceIdType.MESH


def crossing(home):
    away = home // (2 * LOCAL) - lax.axis_index("ep") // 2
    return away * away


def merge(i, crossed, aux, sibling, factors, pieces, p):
    held = i + crossed * (4 - 8 * ((i // 4) % 2))
    delta = lax.dot_general(
        jnp.concatenate([aux[p // 2][held, p % 2], sibling[held, p]], axis=0),
        factors,
        (((0,), (0,)), ((), ())),
        preferred_element_type=jnp.float32,
    )
    raw = [piece[held].astype(jnp.float32) for piece in pieces]
    merged = (raw[0] if len(raw) == 1 else jnp.concatenate(raw, axis=0)) + delta
    most = jnp.max(jnp.max(jnp.abs(merged), axis=0, keepdims=True), axis=1, keepdims=True)
    scale = (most + 1e-6).astype(jnp.bfloat16).astype(jnp.float32)
    return (merged * (1.0 / scale)).astype(jnp.bfloat16), scale


def kernel(active_in, slot_in, gate, up, down, mf, hf, out, scales_out, hf_all, sibling, *refs):
    n = ALL
    kept, refs = refs[: len(LAST_PIECES) + 2], refs[len(LAST_PIECES) + 2 :]
    first = n - len(kept)
    a_bufs, b_bufs, l_bufs = refs[:n], refs[n : 2 * n], refs[2 * n : 2 * n + first] + kept
    (hf_in, hf_wide, hf_rows, active, slot, source,
     a_send, a_recv, b_send, b_recv, c_send, c_recv, in_sem) = refs[2 * n + first :]
    weights = (gate, up, down)

    k, j = lax.axis_index("ep"), lax.axis_index("fsdp")
    h, core = k // 2, k % 2
    y, l, x = j // 8, (j // 4) % 2, j % 4
    flip = 4 - 8 * l

    def partner(d):
        k2 = (k + d) % EP
        dh = k2 // 2 - h
        return k2, j + dh * dh * flip

    def owner(o):
        o = (o * STEP) % OWNERS
        return ((y + o // 8) % 4) * 8 + ((l + (o // 4) % 2) % 2) * 4 + (x + o % 4) % 4

    barrier = pltpu.get_barrier_semaphore()
    for d in range(1, EP):
        pl.semaphore_signal(barrier, inc=1, device_id=partner(d), device_id_type=MESH)

    @pl.loop(1, OWNERS, unroll=True)
    def _(o):
        pl.semaphore_signal(barrier, inc=1, device_id=(k, owner(o)), device_id_type=MESH)

    fetches = [
        pltpu.make_async_copy(src, dst, in_sem.at[q])
        for q, (src, dst) in enumerate(((hf, hf_in), (active_in, active), (slot_in, slot)))
    ]
    for fetch in fetches:
        fetch.start()
    pl.semaphore_wait(barrier, EP - 1 + OWNERS - 1)

    mine = pl.ds(k * LOCAL, LOCAL)

    def a_pairs(c, k2):
        half = pl.ds((k2 % 2) * HALF, HALF)
        if c == AUX:
            return ((mf.at[:, pl.ds(0, 2), half, :], a_bufs[c].at[mine]),)
        if c == AUX + 1:
            return (
                (mf.at[:, pl.ds(2, 1), half, :], a_bufs[c].at[mine, pl.ds(0, 1)]),
                (hf_rows.at[:, pl.ds(k2, 1)], a_bufs[c].at[mine, pl.ds(1, 1)]),
            )
        b, r0, rows = PIECES[c]
        columns = pl.ds(pl.multiple_of(k2 * COLS + (b % NCB) * BLK, BLK), BLK)
        return ((weights[b // NCB].at[:, pl.ds(r0, rows), columns], a_bufs[c].at[mine]),)

    def a_start(c):
        for d in range(1, EP):
            k2, j2 = partner(d)
            for src, dst in a_pairs(c, k2):
                pltpu.make_async_remote_copy(
                    src_ref=src, dst_ref=dst, send_sem=a_send.at[c], recv_sem=a_recv.at[c],
                    device_id=(k2, j2), device_id_type=MESH,
                ).start()
        for src, dst in a_pairs(c, k):
            pltpu.make_async_copy(src, dst, a_recv.at[c]).start()

    def b_start(c):
        a, b, land = a_bufs[c], b_bufs[c], l_bufs[c]

        @pl.loop(0, OWNERS)
        def _(s):
            b[s] = a[source[s]]

        @pl.loop(1, OWNERS)
        def _(o):
            s = owner(o)
            pltpu.make_async_remote_copy(
                src_ref=b.at[s], dst_ref=land.at[j], send_sem=b_send.at[c], recv_sem=b_recv.at[c],
                device_id=(k, s), device_id_type=MESH,
            ).start()

        pltpu.make_async_copy(b.at[j], land.at[j], b_recv.at[c]).start()

    for c in ORDER[:AUX_AT]:
        a_start(c)

    for fetch in fetches:
        fetch.wait()

    @pl.loop(0, LOCAL)
    def _(e):
        factor = (ADAPTER_SCALE * active[e]).astype(jnp.float32)
        for k2 in range(EP):
            hf_wide[k2] = jnp.zeros((HALF, BLK), jnp.float32)
        for p in range(MATS):
            rows = hf_in[e, p].astype(jnp.float32) * factor
            for k2 in range(EP):
                for cb in range(NCB):
                    at = k2 * COLS + cb * BLK
                    hf_wide[k2, pl.ds(2 * (p * NCB + cb), 2), :] = rows[:, at : at + BLK]
        hf_rows[e] = hf_wide[...].astype(jnp.bfloat16)

    for c in ORDER[AUX_AT:]:
        a_start(c)

    @pl.loop(0, OWNERS)
    def _(s):
        found = jnp.int32(0)
        for e in range(EXPERTS):
            found = jnp.where(slot[e] == s, e, found)
        source[s] = found

    crossed = crossing(source[j])

    def sibling_copies():
        return [
            pltpu.make_async_remote_copy(
                src_ref=l_bufs[AUX + q].at[:, pl.ds(0, mats)], dst_ref=sibling.at[:, pl.ds(2 * q, mats)],
                send_sem=c_send.at[q], recv_sem=c_recv.at[q],
                device_id=(k + 1 - 2 * core, j), device_id_type=MESH,
            )
            for q, mats in ((0, 2), (1, 1))
        ]

    def b_wait(c):
        pltpu.make_async_copy(l_bufs[c], l_bufs[c], b_recv.at[c]).wait()

    def factors():
        for c, copy in zip(FACTORS, sibling_copies()):
            b_wait(c)
            copy.start()
        packed = l_bufs[AUX + 1][:, 1].reshape(OWNERS * HALF, BLK)
        row = lax.broadcasted_iota(jnp.int32, (RANK, OWNERS * HALF), 0)
        col = lax.broadcasted_iota(jnp.int32, (RANK, OWNERS * HALF), 1)
        row = (row + core * HALF) % RANK
        holder = row // 2
        holder = holder + crossed * (4 - 8 * ((holder // 4) % 2))
        first = holder * HALF + row % 2
        for p in range(MATS):
            for cb in range(NCB):
                pick = jnp.where(col == first + 2 * (p * NCB + cb), 1.0, 0.0).astype(jnp.bfloat16)
                hf_all[p * NCB + cb] = jnp.dot(pick, packed, preferred_element_type=jnp.float32).astype(jnp.bfloat16)

    lanes = lax.broadcasted_iota(jnp.int32, (1, BLK), 1)

    def compute(b):
        pieces = [c for c in range(AUX) if PIECES[c][0] == b]
        for c in pieces:
            b_wait(c)
        if b == LAST:
            return
        p, columns = b // NCB, slice((b % NCB) * BLK, (b % NCB + 1) * BLK)

        def one(i, scales):
            out[p, i, :, columns], scale = merge(
                i, crossed, l_bufs[AUX:], sibling, hf_all[b], [l_bufs[c] for c in pieces], p
            )
            return jnp.where(lanes == i, scale, scales)

        scales = lax.fori_loop(0, OWNERS, one, jnp.zeros((1, BLK), jnp.float32), unroll=4)
        scales_out[p, pl.ds(b % NCB, 1), :] = scales

    todo = [(max(ORDER.index(c) for c in FACTORS), "factors")]
    todo += [(max(ORDER.index(c) for c in range(AUX) if PIECES[c][0] == b), b) for b in range(BLOCKS)]

    def work(until):
        while todo and todo[0][0] <= until:
            task = todo.pop(0)[1]
            if task == "factors":
                factors()
                continue
            if task == 0:
                for copy in sibling_copies():
                    copy.wait()
            compute(task)

    for at, c in enumerate(ORDER):
        pltpu.make_async_copy(a_bufs[c], a_bufs[c], a_recv.at[c]).wait()
        b_start(c)
        work(at - LAG)

    def b_sent(c):
        given = b_bufs[c].at[pl.ds(0, OWNERS - 1)]
        pltpu.make_async_copy(given, given, b_send.at[c]).wait()

    for c in ORDER:
        given = a_bufs[c].at[pl.ds(0, EXPERTS - LOCAL)]
        pltpu.make_async_copy(given, given, a_send.at[c]).wait()
        if c not in LAST_PIECES:
            b_sent(c)
    work(len(ORDER))
    for c in LAST_PIECES:
        b_sent(c)


def store(slot_in, blocks, scales, hf_all, sibling, *refs):
    pieces, aux = refs[: len(LAST_PIECES)], refs[len(LAST_PIECES) : len(LAST_PIECES) + 2]
    out, scales_out, slot, last, slot_sem, sem = refs[len(LAST_PIECES) + 2 :]
    p, cb = LAST // NCB, LAST % NCB
    copies = []
    fetch = pltpu.make_async_copy(slot_in, slot, slot_sem)
    fetch.start()

    def begin(src, dst):
        copies.append(pltpu.make_async_copy(src, dst, sem.at[len(copies)]))
        copies[-1].start()

    for q in range(MATS):
        for i in range(0, OWNERS, STORE):
            rows = pl.ds(i, STORE)
            if q == p:
                begin(blocks.at[q, rows, :, pl.ds(0, cb * BLK)], out.at[q, rows, :, pl.ds(0, cb * BLK)])
            else:
                begin(blocks.at[q, rows], out.at[q, rows])

    fetch.wait()
    j = lax.axis_index("fsdp")
    home = jnp.int32(0)
    for e in range(EXPERTS):
        home = jnp.where(slot[e] == j, e, home)
    crossed = crossing(home)
    lanes = lax.broadcasted_iota(jnp.int32, (1, BLK), 1)

    def one(i, scales_now):
        last[i], scale = merge(i, crossed, aux, sibling, hf_all[LAST], pieces, p)
        return jnp.where(lanes == i, scale, scales_now)

    final = jnp.zeros((1, BLK), jnp.float32)
    for i in range(0, OWNERS, STORE):
        final = lax.fori_loop(i, i + STORE, one, final, unroll=4)
        rows = pl.ds(i, STORE)
        begin(last.at[rows], out.at[p, rows, :, pl.ds(cb * BLK, BLK)])
    for q in range(MATS):
        scales_out[q] = scales[q, :NCB, :OWNERS].astype(jnp.bfloat16)
    scales_out[p, cb : cb + 1, :] = final[:, :OWNERS].astype(jnp.bfloat16)
    for copy in copies:
        copy.wait()


def on_device(
    gate_weight, up_weight, down_weight, model_factors, hidden_factors, active, expert_rollout_slot
):
    shapes = [(OWNERS, rows, BLK) for _, _, rows in PIECES] + [(OWNERS, 2, HALF, BLK)] * 2
    bufs = [pltpu.VMEM(shape, jnp.bfloat16) for shape in shapes]
    vmem, anywhere = (pl.BlockSpec(memory_space=s) for s in (pltpu.VMEM, pl.ANY))
    sems = pltpu.SemaphoreType.DMA
    n = len(bufs)

    kept = len(LAST_PIECES) + 2
    made = pl.pallas_call(
        kernel,
        out_shape=(
            pltpu.VMEM((MATS, OWNERS, BLK, COLS), jnp.bfloat16),
            pltpu.VMEM((MATS, 8, BLK), jnp.float32),
            pltpu.VMEM((BLOCKS, RANK, BLK), jnp.bfloat16),
            pltpu.VMEM((OWNERS, MATS, HALF, BLK), jnp.bfloat16),
            *bufs[n - kept :],
        ),
        in_specs=[anywhere] * 7,
        out_specs=(vmem,) * (4 + kept),
        scratch_shapes=bufs * 2 + bufs[: n - kept] + [
            pltpu.VMEM((LOCAL, MATS, 2, EP * COLS), jnp.bfloat16),
            pltpu.VMEM((EP, HALF, BLK), jnp.float32),
            pltpu.VMEM((LOCAL, EP, HALF, BLK), jnp.bfloat16),
            pltpu.SMEM((LOCAL,), jnp.int32),
            pltpu.SMEM((EXPERTS,), jnp.int32),
            pltpu.SMEM((EXPERTS,), jnp.int32),
            sems((n,)), sems((n,)), sems((n,)), sems((n,)), sems((2,)), sems((2,)), sems((3,)),
        ],
        compiler_params=pltpu.CompilerParams(
            collective_id=0, has_side_effects=True, vmem_limit_bytes=50 * 1024 * 1024
        ),
    )(active, expert_rollout_slot, gate_weight, up_weight, down_weight, model_factors, hidden_factors)

    quantized, block_scales = pl.pallas_call(
        store,
        out_shape=(
            jax.ShapeDtypeStruct((MATS, OWNERS, BLK, COLS), jnp.bfloat16),
            jax.ShapeDtypeStruct((MATS, NCB, OWNERS), jnp.bfloat16),
        ),
        in_specs=[anywhere, anywhere] + [vmem] * (3 + kept),
        out_specs=(anywhere, vmem),
        scratch_shapes=[pltpu.SMEM((EXPERTS,), jnp.int32), pltpu.VMEM((OWNERS, BLK, BLK), jnp.bfloat16), sems, sems(((MATS + 1) * OWNERS // STORE,))],
        compiler_params=pltpu.CompilerParams(vmem_limit_bytes=8 * 1024 * 1024),
    )(expert_rollout_slot, *made)
    return quantized.reshape(1, MATS, OWNERS * BLK, COLS), block_scales.transpose(0, 2, 1)[None]


def solution(mesh):
    placed = (
        P("ep", "fsdp", None),
        P("ep", "fsdp", None),
        P("ep", "fsdp", None),
        P("ep", None, None, "fsdp"),
        P("ep", None, "fsdp", None),
        P("ep"),
        P(),
    )
    return jax.shard_map(
        on_device,
        mesh=mesh,
        in_specs=placed,
        out_specs=(P("fsdp", None, None, "ep"), P("fsdp", None, None, "ep")),
        check_vma=False,
    )
```

```python
import jax
import jax.numpy as jnp
from jax import lax
from jax.experimental import pallas as pl
from jax.experimental.pallas import tpu as pltpu
from jax.sharding import PartitionSpec as P

BLK = 128
ADAPTER_SCALE = 2
EP = 4
OWNERS = 32
LOCAL = 8
EXPERTS = EP * LOCAL
MATS = 3
RANK = 64
HALF = RANK // 2
COLS = 384
NCB = COLS // BLK
BLOCKS = MATS * NCB
ROWS = ((48, 48, 32),) * 9
PIECES = tuple(
    (b, sum(cut[:i]), rows) for b, cut in enumerate(ROWS) for i, rows in enumerate(cut)
)
AUX = len(PIECES)
FACTORS = tuple(range(AUX, AUX + MATS + 1))
ALL = AUX + len(FACTORS)
AUX_AT = 2
ORDER = tuple(range(AUX_AT)) + FACTORS + tuple(range(AUX_AT, AUX))
LAG = 4
LAST = BLOCKS - 1
LAST_PIECES = tuple(c for c in range(AUX) if PIECES[c][0] == LAST)
STORE = 8
STEP = 13
MESH = pl.DeviceIdType.MESH


def crossing(home):
    away = home // (2 * LOCAL) - lax.axis_index("ep") // 2
    return away * away


def merge(i, crossed, aux, sibling, factors, pieces, p):
    held = i + crossed * (4 - 8 * ((i // 4) % 2))
    delta = lax.dot_general(
        jnp.concatenate([aux[p][held, 0], sibling[held, p]], axis=0),
        factors,
        (((0,), (0,)), ((), ())),
        preferred_element_type=jnp.float32,
    )
    raw = [piece[held].astype(jnp.float32) for piece in pieces]
    merged = (raw[0] if len(raw) == 1 else jnp.concatenate(raw, axis=0)) + delta
    most = jnp.max(jnp.max(jnp.abs(merged), axis=0, keepdims=True), axis=1, keepdims=True)
    scale = (most + 1e-6).astype(jnp.bfloat16).astype(jnp.float32)
    return (merged * (1.0 / scale)).astype(jnp.bfloat16), scale


def kernel(active_in, slot_in, gate, up, down, mf, hf, out, scales_out, hf_all, sibling, *refs):
    n = ALL
    kept, refs = refs[: len(LAST_PIECES + FACTORS)], refs[len(LAST_PIECES + FACTORS) :]
    first = n - len(kept)
    a_bufs, b_bufs, l_bufs = refs[:n], refs[n : 2 * n], refs[2 * n : 2 * n + first] + kept
    (hf_in, hf_wide, hf_rows, active, slot, source,
     a_send, a_recv, b_send, b_recv, c_send, c_recv, in_sem) = refs[2 * n + first :]
    weights = (gate, up, down)

    k, j = lax.axis_index("ep"), lax.axis_index("fsdp")
    h, core = k // 2, k % 2
    y, l, x = j // 8, (j // 4) % 2, j % 4
    flip = 4 - 8 * l

    def partner(d):
        k2 = (k + d) % EP
        dh = k2 // 2 - h
        return k2, j + dh * dh * flip

    def owner(o):
        o = lax.rem(o * STEP, OWNERS)
        dx = lax.rem(o, 4)
        dl = lax.rem(lax.div(o, 4), 2)
        return lax.rem(y + lax.div(o, 8), 4) * 8 + lax.rem(l + dl, 2) * 4 + lax.rem(x + dx, 4)

    barrier = pltpu.get_barrier_semaphore()
    for d in range(1, EP):
        pl.semaphore_signal(barrier, inc=1, device_id=partner(d), device_id_type=MESH)

    @pl.loop(1, OWNERS, unroll=True)
    def _(o):
        pl.semaphore_signal(barrier, inc=1, device_id=(k, owner(o)), device_id_type=MESH)

    fetches = [
        pltpu.make_async_copy(src, dst, in_sem.at[q])
        for q, (src, dst) in enumerate(((hf, hf_in), (active_in, active), (slot_in, slot)))
    ]
    for fetch in fetches:
        fetch.start()
    pl.semaphore_wait(barrier, EP - 1 + OWNERS - 1)

    mine = pl.ds(k * LOCAL, LOCAL)

    def a_pairs(c, k2):
        half = pl.ds((k2 % 2) * HALF, HALF)
        if c == FACTORS[-1]:
            return ((hf_rows.at[:, pl.ds(k2, 1)], a_bufs[c].at[mine]),)
        if c in FACTORS:
            return ((mf.at[:, pl.ds(c - AUX, 1), half, :], a_bufs[c].at[mine]),)
        b, r0, rows = PIECES[c]
        columns = pl.ds(pl.multiple_of(k2 * COLS + (b % NCB) * BLK, BLK), BLK)
        return ((weights[b // NCB].at[:, pl.ds(r0, rows), columns], a_bufs[c].at[mine]),)

    def a_start(c):
        for d in range(1, EP):
            k2, j2 = partner(d)
            for src, dst in a_pairs(c, k2):
                pltpu.make_async_remote_copy(
                    src_ref=src, dst_ref=dst, send_sem=a_send.at[c], recv_sem=a_recv.at[c],
                    device_id=(k2, j2), device_id_type=MESH,
                ).start()
        for src, dst in a_pairs(c, k):
            pltpu.make_async_copy(src, dst, a_recv.at[c]).start()

    def b_start(c):
        a, b, land = a_bufs[c], b_bufs[c], l_bufs[c]

        @pl.loop(0, OWNERS)
        def _(s):
            b[s] = a[source[s]]

        @pl.loop(1, OWNERS)
        def _(o):
            s = owner(o)
            pltpu.make_async_remote_copy(
                src_ref=b.at[s], dst_ref=land.at[j], send_sem=b_send.at[c], recv_sem=b_recv.at[c],
                device_id=(k, s), device_id_type=MESH,
            ).start()

        pltpu.make_async_copy(b.at[j], land.at[j], b_recv.at[c]).start()

    for c in ORDER[:AUX_AT]:
        a_start(c)

    for fetch in fetches:
        fetch.wait()

    @pl.loop(0, LOCAL)
    def _(e):
        factor = (ADAPTER_SCALE * active[e]).astype(jnp.float32)
        for k2 in range(EP):
            hf_wide[k2] = jnp.zeros((HALF, BLK), jnp.float32)
        for p in range(MATS):
            rows = hf_in[e, p].astype(jnp.float32) * factor
            for k2 in range(EP):
                for cb in range(NCB):
                    at = k2 * COLS + cb * BLK
                    hf_wide[k2, pl.ds(2 * (p * NCB + cb), 2), :] = rows[:, at : at + BLK]
        hf_rows[e] = hf_wide[...].astype(jnp.bfloat16)

    for c in ORDER[AUX_AT:]:
        a_start(c)

    @pl.loop(0, OWNERS)
    def _(s):
        found = jnp.int32(0)
        for e in range(EXPERTS):
            found = jnp.where(slot[e] == s, e, found)
        source[s] = found

    crossed = crossing(source[j])

    def sibling_copies():
        return [
            pltpu.make_async_remote_copy(
                src_ref=l_bufs[AUX + q], dst_ref=sibling.at[:, pl.ds(q, 1)],
                send_sem=c_send.at[q], recv_sem=c_recv.at[q],
                device_id=(k + 1 - 2 * core, j), device_id_type=MESH,
            )
            for q in range(MATS)
        ]

    def b_wait(c):
        pltpu.make_async_copy(l_bufs[c], l_bufs[c], b_recv.at[c]).wait()

    def factors():
        for c, copy in zip(FACTORS, sibling_copies()):
            b_wait(c)
            copy.start()
        b_wait(FACTORS[-1])
        packed = l_bufs[FACTORS[-1]][:, 0].reshape(OWNERS * HALF, BLK)
        row = lax.broadcasted_iota(jnp.int32, (RANK, OWNERS * HALF), 0)
        col = lax.broadcasted_iota(jnp.int32, (RANK, OWNERS * HALF), 1)
        row = (row + core * HALF) % RANK
        holder = row // 2
        holder = holder + crossed * (4 - 8 * ((holder // 4) % 2))
        first = holder * HALF + row % 2
        for p in range(MATS):
            for cb in range(NCB):
                pick = jnp.where(col == first + 2 * (p * NCB + cb), 1.0, 0.0).astype(jnp.bfloat16)
                hf_all[p * NCB + cb] = jnp.dot(pick, packed, preferred_element_type=jnp.float32).astype(jnp.bfloat16)

    lanes = lax.broadcasted_iota(jnp.int32, (1, BLK), 1)

    def compute(b):
        pieces = [c for c in range(AUX) if PIECES[c][0] == b]
        for c in pieces:
            b_wait(c)
        if b == LAST:
            return
        p, columns = b // NCB, slice((b % NCB) * BLK, (b % NCB + 1) * BLK)

        def one(i, scales):
            out[p, i, :, columns], scale = merge(
                i, crossed, l_bufs[AUX:], sibling, hf_all[b], [l_bufs[c] for c in pieces], p
            )
            return jnp.where(lanes == i, scale, scales)

        scales = lax.fori_loop(0, OWNERS, one, jnp.zeros((1, BLK), jnp.float32), unroll=4)
        scales_out[p, pl.ds(b % NCB, 1), :] = scales

    todo = [(max(ORDER.index(c) for c in FACTORS), "factors")]
    todo += [(max(ORDER.index(c) for c in range(AUX) if PIECES[c][0] == b), b) for b in range(BLOCKS)]

    def work(until):
        while todo and todo[0][0] <= until:
            task = todo.pop(0)[1]
            if task == "factors":
                factors()
                continue
            if task == 0:
                for copy in sibling_copies():
                    copy.wait()
            compute(task)

    for at, c in enumerate(ORDER):
        pltpu.make_async_copy(a_bufs[c], a_bufs[c], a_recv.at[c]).wait()
        b_start(c)
        work(at - LAG)

    def b_sent(c):
        given = b_bufs[c].at[pl.ds(0, OWNERS - 1)]
        pltpu.make_async_copy(given, given, b_send.at[c]).wait()

    for c in ORDER:
        given = a_bufs[c].at[pl.ds(0, EXPERTS - LOCAL)]
        pltpu.make_async_copy(given, given, a_send.at[c]).wait()
        if c not in LAST_PIECES:
            b_sent(c)
    work(len(ORDER))
    for c in LAST_PIECES:
        b_sent(c)


def store(slot_in, blocks, scales, hf_all, sibling, *refs):
    pieces, aux = refs[: len(LAST_PIECES)], refs[len(LAST_PIECES) : len(LAST_PIECES + FACTORS)]
    out, scales_out, slot, last, slot_sem, sem = refs[len(LAST_PIECES + FACTORS) :]
    p, cb = LAST // NCB, LAST % NCB
    copies = []
    fetch = pltpu.make_async_copy(slot_in, slot, slot_sem)
    fetch.start()

    def begin(src, dst):
        copies.append(pltpu.make_async_copy(src, dst, sem.at[len(copies)]))
        copies[-1].start()

    for q in range(MATS):
        for i in range(0, OWNERS, STORE):
            rows = pl.ds(i, STORE)
            if q == p:
                begin(blocks.at[q, rows, :, pl.ds(0, cb * BLK)], out.at[q, rows, :, pl.ds(0, cb * BLK)])
            else:
                begin(blocks.at[q, rows], out.at[q, rows])

    fetch.wait()
    j = lax.axis_index("fsdp")
    home = jnp.int32(0)
    for e in range(EXPERTS):
        home = jnp.where(slot[e] == j, e, home)
    crossed = crossing(home)
    lanes = lax.broadcasted_iota(jnp.int32, (1, BLK), 1)

    def one(i, scales_now):
        last[i], scale = merge(i, crossed, aux, sibling, hf_all[LAST], pieces, p)
        return jnp.where(lanes == i, scale, scales_now)

    final = jnp.zeros((1, BLK), jnp.float32)
    for i in range(0, OWNERS, STORE):
        final = lax.fori_loop(i, i + STORE, one, final, unroll=4)
        rows = pl.ds(i, STORE)
        begin(last.at[rows], out.at[p, rows, :, pl.ds(cb * BLK, BLK)])
    for q in range(MATS):
        scales_out[q] = scales[q, :NCB, :OWNERS].astype(jnp.bfloat16)
    scales_out[p, cb : cb + 1, :] = final[:, :OWNERS].astype(jnp.bfloat16)
    for copy in copies:
        copy.wait()


def on_device(
    gate_weight, up_weight, down_weight, model_factors, hidden_factors, active, expert_rollout_slot
):
    shapes = [(OWNERS, rows, BLK) for _, _, rows in PIECES] + [(OWNERS, 1, HALF, BLK)] * len(FACTORS)
    bufs = [pltpu.VMEM(shape, jnp.bfloat16) for shape in shapes]
    vmem, anywhere = (pl.BlockSpec(memory_space=s) for s in (pltpu.VMEM, pl.ANY))
    sems = pltpu.SemaphoreType.DMA
    n = len(bufs)

    kept = len(LAST_PIECES + FACTORS)
    made = pl.pallas_call(
        kernel,
        out_shape=(
            pltpu.VMEM((MATS, OWNERS, BLK, COLS), jnp.bfloat16),
            pltpu.VMEM((MATS, 8, BLK), jnp.float32),
            pltpu.VMEM((BLOCKS, RANK, BLK), jnp.bfloat16),
            pltpu.VMEM((OWNERS, MATS, HALF, BLK), jnp.bfloat16),
            *bufs[n - kept :],
        ),
        in_specs=[anywhere] * 7,
        out_specs=(vmem,) * (4 + kept),
        scratch_shapes=bufs * 2 + bufs[: n - kept] + [
            pltpu.VMEM((LOCAL, MATS, 2, EP * COLS), jnp.bfloat16),
            pltpu.VMEM((EP, HALF, BLK), jnp.float32),
            pltpu.VMEM((LOCAL, EP, HALF, BLK), jnp.bfloat16),
            pltpu.SMEM((LOCAL,), jnp.int32),
            pltpu.SMEM((EXPERTS,), jnp.int32),
            pltpu.SMEM((EXPERTS,), jnp.int32),
            sems((n,)), sems((n,)), sems((n,)), sems((n,)), sems((MATS,)), sems((MATS,)), sems((3,)),
        ],
        compiler_params=pltpu.CompilerParams(
            collective_id=0, has_side_effects=True, vmem_limit_bytes=50 * 1024 * 1024
        ),
    )(active, expert_rollout_slot, gate_weight, up_weight, down_weight, model_factors, hidden_factors)

    quantized, block_scales = pl.pallas_call(
        store,
        out_shape=(
            jax.ShapeDtypeStruct((MATS, OWNERS, BLK, COLS), jnp.bfloat16),
            jax.ShapeDtypeStruct((MATS, NCB, OWNERS), jnp.bfloat16),
        ),
        in_specs=[anywhere, anywhere] + [vmem] * (3 + kept),
        out_specs=(anywhere, vmem),
        scratch_shapes=[pltpu.SMEM((EXPERTS,), jnp.int32), pltpu.VMEM((OWNERS, BLK, BLK), jnp.bfloat16), sems, sems(((MATS + 1) * OWNERS // STORE,))],
        compiler_params=pltpu.CompilerParams(vmem_limit_bytes=8 * 1024 * 1024),
    )(expert_rollout_slot, *made)
    return quantized.reshape(1, MATS, OWNERS * BLK, COLS), block_scales.transpose(0, 2, 1)[None]


def solution(mesh):
    placed = (
        P("ep", "fsdp", None),
        P("ep", "fsdp", None),
        P("ep", "fsdp", None),
        P("ep", None, None, "fsdp"),
        P("ep", None, "fsdp", None),
        P("ep"),
        P(),
    )
    return jax.shard_map(
        on_device,
        mesh=mesh,
        in_specs=placed,
        out_specs=(P("fsdp", None, None, "ep"), P("fsdp", None, None, "ep")),
        check_vma=False,
    )
```

```python
import jax
import jax.numpy as jnp
from jax import lax
from jax.experimental import pallas as pl
from jax.experimental.pallas import tpu as pltpu
from jax.sharding import PartitionSpec as P

BLK = 128
ADAPTER_SCALE = 2
EP = 4
OWNERS = 32
LOCAL = 8
EXPERTS = EP * LOCAL
MATS = 3
RANK = 64
HALF = RANK // 2
COLS = 384
NCB = COLS // BLK
BLOCKS = MATS * NCB
ROWS = ((48, 48, 32),) * 9
PIECES = tuple(
    (b, sum(cut[:i]), rows) for b, cut in enumerate(ROWS) for i, rows in enumerate(cut)
)
AUX = len(PIECES)
FACTORS = tuple(range(AUX, AUX + MATS + 1))
ALL = AUX + len(FACTORS)
AUX_AT = 2
ORDER = tuple(range(AUX_AT)) + FACTORS + tuple(range(AUX_AT, AUX))
LAG = 4
LAST = BLOCKS - 1
LAST_PIECES = tuple(c for c in range(AUX) if PIECES[c][0] == LAST)
STORE = 8
STEP = 13
MESH = pl.DeviceIdType.MESH


def crossing(home):
    away = home // (2 * LOCAL) - lax.axis_index("ep") // 2
    return away * away


def merge(i, crossed, aux, sibling, factors, pieces, p):
    held = i + crossed * (4 - 8 * ((i // 4) % 2))
    delta = lax.dot_general(
        jnp.concatenate([aux[p][held, 0], sibling[held, p]], axis=0),
        factors,
        (((0,), (0,)), ((), ())),
        preferred_element_type=jnp.float32,
    )
    raw = [piece[held].astype(jnp.float32) for piece in pieces]
    merged = (raw[0] if len(raw) == 1 else jnp.concatenate(raw, axis=0)) + delta
    most = jnp.max(jnp.max(jnp.abs(merged), axis=0, keepdims=True), axis=1, keepdims=True)
    scale = (most + 1e-6).astype(jnp.bfloat16).astype(jnp.float32)
    return (merged * (1.0 / scale)).astype(jnp.bfloat16), scale


def kernel(active_in, slot_in, gate, up, down, mf, hf, out, scales_out, hf_all, sibling, *refs):
    n = ALL
    kept, refs = refs[: len(LAST_PIECES + FACTORS)], refs[len(LAST_PIECES + FACTORS) :]
    first = n - len(kept)
    a_bufs, b_bufs, l_bufs = refs[:n], refs[n : 2 * n], refs[2 * n : 2 * n + first] + kept
    (hf_in, hf_wide, hf_rows, active, slot, source,
     a_send, a_recv, b_send, b_recv, c_send, c_recv, in_sem) = refs[2 * n + first :]
    weights = (gate, up, down)

    k, j = lax.axis_index("ep"), lax.axis_index("fsdp")
    h, core = k // 2, k % 2
    y, l, x = j // 8, (j // 4) % 2, j % 4
    flip = 4 - 8 * l

    def partner(d):
        k2 = (k + d) % EP
        dh = k2 // 2 - h
        return k2, j + dh * dh * flip

    def owner(o):
        o = lax.rem(o * STEP, OWNERS)
        dx = lax.rem(o, 4)
        dl = lax.rem(lax.div(o, 4), 2)
        return lax.rem(y + lax.div(o, 8), 4) * 8 + lax.rem(l + dl, 2) * 4 + lax.rem(x + dx, 4)

    barrier = pltpu.get_barrier_semaphore()
    for d in range(1, EP):
        pl.semaphore_signal(barrier, inc=1, device_id=partner(d), device_id_type=MESH)

    @pl.loop(1, OWNERS, unroll=True)
    def _(o):
        pl.semaphore_signal(barrier, inc=1, device_id=(k, owner(o)), device_id_type=MESH)

    fetches = [
        pltpu.make_async_copy(src, dst, in_sem.at[q])
        for q, (src, dst) in enumerate(((hf, hf_in), (active_in, active), (slot_in, slot)))
    ]
    for fetch in fetches:
        fetch.start()
    pl.semaphore_wait(barrier, EP - 1 + OWNERS - 1)

    mine = pl.ds(k * LOCAL, LOCAL)

    def a_pairs(c, k2):
        half = pl.ds((k2 % 2) * HALF, HALF)
        if c == FACTORS[-1]:
            return ((hf_rows.at[:, pl.ds(k2, 1)], a_bufs[c].at[mine]),)
        if c in FACTORS:
            return ((mf.at[:, pl.ds(c - AUX, 1), half, :], a_bufs[c].at[mine]),)
        b, r0, rows = PIECES[c]
        columns = pl.ds(pl.multiple_of(k2 * COLS + (b % NCB) * BLK, BLK), BLK)
        return ((weights[b // NCB].at[:, pl.ds(r0, rows), columns], a_bufs[c].at[mine]),)

    def a_start(c):
        for d in range(1, EP):
            k2, j2 = partner(d)
            for src, dst in a_pairs(c, k2):
                pltpu.make_async_remote_copy(
                    src_ref=src, dst_ref=dst, send_sem=a_send.at[c], recv_sem=a_recv.at[c],
                    device_id=(k2, j2), device_id_type=MESH,
                ).start()
        for src, dst in a_pairs(c, k):
            pltpu.make_async_copy(src, dst, a_recv.at[c]).start()

    def b_start(c):
        a, b, land = a_bufs[c], b_bufs[c], l_bufs[c]

        @pl.loop(1, OWNERS)
        def _(o):
            s = owner(o)
            b[s] = a[source[s]]
            pltpu.make_async_remote_copy(
                src_ref=b.at[s], dst_ref=land.at[j], send_sem=b_send.at[c], recv_sem=b_recv.at[c],
                device_id=(k, s), device_id_type=MESH,
            ).start()

        b[j] = a[source[j]]
        pltpu.make_async_copy(b.at[j], land.at[j], b_recv.at[c]).start()

    for c in ORDER[:AUX_AT]:
        a_start(c)

    for fetch in fetches:
        fetch.wait()

    @pl.loop(0, LOCAL)
    def _(e):
        factor = (ADAPTER_SCALE * active[e]).astype(jnp.float32)
        for k2 in range(EP):
            hf_wide[k2] = jnp.zeros((HALF, BLK), jnp.float32)
        for p in range(MATS):
            rows = hf_in[e, p].astype(jnp.float32) * factor
            for k2 in range(EP):
                for cb in range(NCB):
                    at = k2 * COLS + cb * BLK
                    hf_wide[k2, pl.ds(2 * (p * NCB + cb), 2), :] = rows[:, at : at + BLK]
        hf_rows[e] = hf_wide[...].astype(jnp.bfloat16)

    for c in ORDER[AUX_AT:]:
        a_start(c)

    @pl.loop(0, OWNERS)
    def _(s):
        found = jnp.int32(0)
        for e in range(EXPERTS):
            found = jnp.where(slot[e] == s, e, found)
        source[s] = found

    crossed = crossing(source[j])

    def sibling_copies():
        return [
            pltpu.make_async_remote_copy(
                src_ref=l_bufs[AUX + q], dst_ref=sibling.at[:, pl.ds(q, 1)],
                send_sem=c_send.at[q], recv_sem=c_recv.at[q],
                device_id=(k + 1 - 2 * core, j), device_id_type=MESH,
            )
            for q in range(MATS)
        ]

    def b_wait(c):
        pltpu.make_async_copy(l_bufs[c], l_bufs[c], b_recv.at[c]).wait()

    def factors():
        for c, copy in zip(FACTORS, sibling_copies()):
            b_wait(c)
            copy.start()
        b_wait(FACTORS[-1])
        packed = l_bufs[FACTORS[-1]][:, 0].reshape(OWNERS * HALF, BLK)
        row = lax.broadcasted_iota(jnp.int32, (RANK, OWNERS * HALF), 0)
        col = lax.broadcasted_iota(jnp.int32, (RANK, OWNERS * HALF), 1)
        row = (row + core * HALF) % RANK
        holder = row // 2
        holder = holder + crossed * (4 - 8 * ((holder // 4) % 2))
        first = holder * HALF + row % 2
        for p in range(MATS):
            for cb in range(NCB):
                pick = jnp.where(col == first + 2 * (p * NCB + cb), 1.0, 0.0).astype(jnp.bfloat16)
                hf_all[p * NCB + cb] = jnp.dot(pick, packed, preferred_element_type=jnp.float32).astype(jnp.bfloat16)

    lanes = lax.broadcasted_iota(jnp.int32, (1, BLK), 1)

    def compute(b):
        pieces = [c for c in range(AUX) if PIECES[c][0] == b]
        for c in pieces:
            b_wait(c)
        if b == LAST:
            return
        p, columns = b // NCB, slice((b % NCB) * BLK, (b % NCB + 1) * BLK)

        def one(i, scales):
            out[p, i, :, columns], scale = merge(
                i, crossed, l_bufs[AUX:], sibling, hf_all[b], [l_bufs[c] for c in pieces], p
            )
            return jnp.where(lanes == i, scale, scales)

        scales = lax.fori_loop(0, OWNERS, one, jnp.zeros((1, BLK), jnp.float32), unroll=4)
        scales_out[p, pl.ds(b % NCB, 1), :] = scales

    todo = [(max(ORDER.index(c) for c in FACTORS), "factors")]
    todo += [(max(ORDER.index(c) for c in range(AUX) if PIECES[c][0] == b), b) for b in range(BLOCKS)]

    def work(until):
        while todo and todo[0][0] <= until:
            task = todo.pop(0)[1]
            if task == "factors":
                factors()
                continue
            if task == 0:
                for copy in sibling_copies():
                    copy.wait()
            compute(task)

    for at, c in enumerate(ORDER):
        pltpu.make_async_copy(a_bufs[c], a_bufs[c], a_recv.at[c]).wait()
        b_start(c)
        work(at - LAG)

    def b_sent(c):
        given = b_bufs[c].at[pl.ds(0, OWNERS - 1)]
        pltpu.make_async_copy(given, given, b_send.at[c]).wait()

    for c in ORDER:
        given = a_bufs[c].at[pl.ds(0, EXPERTS - LOCAL)]
        pltpu.make_async_copy(given, given, a_send.at[c]).wait()
        if c not in LAST_PIECES:
            b_sent(c)
    work(len(ORDER))
    for c in LAST_PIECES:
        b_sent(c)


def store(slot_in, blocks, scales, hf_all, sibling, *refs):
    pieces, aux = refs[: len(LAST_PIECES)], refs[len(LAST_PIECES) : len(LAST_PIECES + FACTORS)]
    out, scales_out, slot, last, slot_sem, sem = refs[len(LAST_PIECES + FACTORS) :]
    p, cb = LAST // NCB, LAST % NCB
    copies = []
    fetch = pltpu.make_async_copy(slot_in, slot, slot_sem)
    fetch.start()

    def begin(src, dst):
        copies.append(pltpu.make_async_copy(src, dst, sem.at[len(copies)]))
        copies[-1].start()

    for q in range(MATS):
        for i in range(0, OWNERS, STORE):
            rows = pl.ds(i, STORE)
            if q == p:
                begin(blocks.at[q, rows, :, pl.ds(0, cb * BLK)], out.at[q, rows, :, pl.ds(0, cb * BLK)])
            else:
                begin(blocks.at[q, rows], out.at[q, rows])

    fetch.wait()
    j = lax.axis_index("fsdp")
    home = jnp.int32(0)
    for e in range(EXPERTS):
        home = jnp.where(slot[e] == j, e, home)
    crossed = crossing(home)
    lanes = lax.broadcasted_iota(jnp.int32, (1, BLK), 1)

    def one(i, scales_now):
        last[i], scale = merge(i, crossed, aux, sibling, hf_all[LAST], pieces, p)
        return jnp.where(lanes == i, scale, scales_now)

    final = jnp.zeros((1, BLK), jnp.float32)
    for i in range(0, OWNERS, STORE):
        final = lax.fori_loop(i, i + STORE, one, final, unroll=4)
        rows = pl.ds(i, STORE)
        begin(last.at[rows], out.at[p, rows, :, pl.ds(cb * BLK, BLK)])
    for q in range(MATS):
        scales_out[q] = scales[q, :NCB, :OWNERS].astype(jnp.bfloat16)
    scales_out[p, cb : cb + 1, :] = final[:, :OWNERS].astype(jnp.bfloat16)
    for copy in copies:
        copy.wait()


def on_device(
    gate_weight, up_weight, down_weight, model_factors, hidden_factors, active, expert_rollout_slot
):
    shapes = [(OWNERS, rows, BLK) for _, _, rows in PIECES] + [(OWNERS, 1, HALF, BLK)] * len(FACTORS)
    bufs = [pltpu.VMEM(shape, jnp.bfloat16) for shape in shapes]
    vmem, anywhere = (pl.BlockSpec(memory_space=s) for s in (pltpu.VMEM, pl.ANY))
    sems = pltpu.SemaphoreType.DMA
    n = len(bufs)

    kept = len(LAST_PIECES + FACTORS)
    made = pl.pallas_call(
        kernel,
        out_shape=(
            pltpu.VMEM((MATS, OWNERS, BLK, COLS), jnp.bfloat16),
            pltpu.VMEM((MATS, 8, BLK), jnp.float32),
            pltpu.VMEM((BLOCKS, RANK, BLK), jnp.bfloat16),
            pltpu.VMEM((OWNERS, MATS, HALF, BLK), jnp.bfloat16),
            *bufs[n - kept :],
        ),
        in_specs=[anywhere] * 7,
        out_specs=(vmem,) * (4 + kept),
        scratch_shapes=bufs * 2 + bufs[: n - kept] + [
            pltpu.VMEM((LOCAL, MATS, 2, EP * COLS), jnp.bfloat16),
            pltpu.VMEM((EP, HALF, BLK), jnp.float32),
            pltpu.VMEM((LOCAL, EP, HALF, BLK), jnp.bfloat16),
            pltpu.SMEM((LOCAL,), jnp.int32),
            pltpu.SMEM((EXPERTS,), jnp.int32),
            pltpu.SMEM((EXPERTS,), jnp.int32),
            sems((n,)), sems((n,)), sems((n,)), sems((n,)), sems((MATS,)), sems((MATS,)), sems((3,)),
        ],
        compiler_params=pltpu.CompilerParams(
            collective_id=0, has_side_effects=True, vmem_limit_bytes=50 * 1024 * 1024
        ),
    )(active, expert_rollout_slot, gate_weight, up_weight, down_weight, model_factors, hidden_factors)

    quantized, block_scales = pl.pallas_call(
        store,
        out_shape=(
            jax.ShapeDtypeStruct((MATS, OWNERS, BLK, COLS), jnp.bfloat16),
            jax.ShapeDtypeStruct((MATS, NCB, OWNERS), jnp.bfloat16),
        ),
        in_specs=[anywhere, anywhere] + [vmem] * (3 + kept),
        out_specs=(anywhere, vmem),
        scratch_shapes=[pltpu.SMEM((EXPERTS,), jnp.int32), pltpu.VMEM((OWNERS, BLK, BLK), jnp.bfloat16), sems, sems(((MATS + 1) * OWNERS // STORE,))],
        compiler_params=pltpu.CompilerParams(vmem_limit_bytes=8 * 1024 * 1024),
    )(expert_rollout_slot, *made)
    return quantized.reshape(1, MATS, OWNERS * BLK, COLS), block_scales.transpose(0, 2, 1)[None]


def solution(mesh):
    placed = (
        P("ep", "fsdp", None),
        P("ep", "fsdp", None),
        P("ep", "fsdp", None),
        P("ep", None, None, "fsdp"),
        P("ep", None, "fsdp", None),
        P("ep"),
        P(),
    )
    return jax.shard_map(
        on_device,
        mesh=mesh,
        in_specs=placed,
        out_specs=(P("fsdp", None, None, "ep"), P("fsdp", None, None, "ep")),
        check_vma=False,
    )
```
